128 devices in a mesh: row: 8 (over x, core), col: 16 (over y, z).
Axes of the slice: x: 4, y: 4, z: 4, core: 2. Of those that a mesh axis runs over, the one named last changes fastest.
Arguments:
- images: bfloat16 [16384, 768], P(('row', 'col')), may hold values from -192 to 192
- texts: bfloat16 [16384, 768], P(('col', 'row')), may hold values from -192 to 192
- log_scale: float32 [], replicated, may hold values from 3 to 5.3
Outputs:
- grad_images: float32 [16384, 768], P(('row', 'col'))
- grad_texts: float32 [16384, 768], P(('col', 'row'))
- loss: float32 [], replicated
- grad_log_scale: float32 [], replicated
The draws below stay inside these ranges and needn't reach their ends.
All inputs are finite; a program needn't handle non-finite values.
Results may differ from the reference program's by a relative error of at most 0.012.
The reference program's roundings to bfloat16 on the way (of `image_low`, `text_low` and `delta_low`) count: a program that leaves them out, or rounds other values in their place, can miss the bound.
Values may be sent and summed in bfloat16 or wider, within the bound.
A program may use at most 64 MiB of HBM per device.

```python
import math
import jax
import jax.numpy as jnp
from jax import lax

E = 768
ROWS_DEV = 128
BATCH = 16384
N_COL = 16


def pair_parts(key, common, anti_share, twin_share, spread):
    shape = (BATCH, E)
    base = jnp.clip(jax.random.normal(jax.random.fold_in(key, 201), shape, jnp.float32), -6.0, 6.0)
    fresh = jnp.clip(jax.random.normal(jax.random.fold_in(key, 202), shape, jnp.float32), -6.0, 6.0)
    shared = jnp.clip(jax.random.normal(jax.random.fold_in(key, 203), (1, E), jnp.float32), -6.0, 6.0)
    level = jax.random.uniform(jax.random.fold_in(key, 204), (BATCH, 1), jnp.float32)
    cosine = jnp.exp(math.log(0.03) + level * math.log(0.95 / 0.03))
    strong = jax.random.uniform(jax.random.fold_in(key, 205), (BATCH, 1), jnp.float32) < 0.05
    cosine = jnp.where(strong, 0.99, cosine)
    twin_pick = jax.random.uniform(jax.random.fold_in(key, 206), (BATCH // 2, 1), jnp.float32) < twin_share
    paired = base.reshape(BATCH // 2, 2, E)
    even_rows = paired[:, 0, :]
    odd_rows = jnp.where(twin_pick, even_rows + 0.15 * paired[:, 1, :], paired[:, 1, :])
    base = jnp.stack([even_rows, odd_rows], axis=1).reshape(BATCH, E)
    twin_rows = jnp.repeat(twin_pick, 2, axis=0)
    cosine = jnp.where(twin_rows, 0.99, cosine)
    anti = jax.random.uniform(jax.random.fold_in(key, 207), (BATCH, 1), jnp.float32) < anti_share
    base = jnp.where(anti, 0.2 * base - shared, base)
    cosine = jnp.where(anti, 0.05, cosine)
    text_dir = math.sqrt(1.0 - common * common) * (cosine * base + jnp.sqrt(1.0 - cosine * cosine) * fresh) + common * shared
    image_scale = jnp.exp(spread * jax.random.uniform(jax.random.fold_in(key, 208), (BATCH, 1), jnp.float32))
    text_scale = jnp.exp(spread * jax.random.uniform(jax.random.fold_in(key, 209), (BATCH, 1), jnp.float32))
    return (base * image_scale, text_dir * text_scale)


def draw_images(key, part):
    made = pair_parts(key, 0.35, 0.0, 0.05, math.log(10.0))
    return made[0].astype(jnp.bfloat16)


def draw_texts(key, part):
    made = pair_parts(key, 0.35, 0.0, 0.05, math.log(10.0))
    return made[1].astype(jnp.bfloat16)


def draw_log_scale(key, part):
    key = jax.random.fold_in(key, 9)
    return jax.random.uniform(key, (), jnp.float32, 3.0, 5.3)


def setup_inputs(seed: int = 0) -> dict:
    arg_keys = jax.random.split(jax.random.key(seed), 4)
    return {
        "images": draw_images(jax.random.fold_in(arg_keys[3], 71), 0),
        "texts": draw_texts(jax.random.fold_in(arg_keys[3], 71), 0),
        "log_scale": draw_log_scale(jax.random.fold_in(arg_keys[3], 71), 0),
    }


EPS = 1e-06

def unit_rows(values):
    full = values.astype(jnp.float32)
    inverse = lax.rsqrt(lax.optimization_barrier(jnp.sum(full * full, axis=1, keepdims=True)) + EPS)
    return (full * inverse, inverse)

def reference(images, texts, log_scale):
    scale = jnp.exp(log_scale)
    image_unit, image_inv = unit_rows(images)
    text_unit, text_inv = unit_rows(texts)
    image_low = image_unit.astype(jnp.bfloat16)
    text_low = text_unit.astype(jnp.bfloat16)
    block = ROWS_DEV * N_COL
    count = BATCH // block
    image_blocks = image_low.reshape(count, block, E)

    def first(carry, piece):
        peak, total = carry
        logits = scale * jnp.dot(piece, text_low.T, preferred_element_type=jnp.float32)
        row_lse = jax.nn.logsumexp(logits, axis=1)
        newpeak = jnp.maximum(peak, lax.optimization_barrier(jnp.max(logits, axis=0)))
        total = total * jnp.exp(peak - newpeak) + lax.optimization_barrier(jnp.sum(jnp.exp(logits - newpeak[None, :]), axis=0))
        return ((newpeak, total), row_lse)
    start_peak = jnp.full((BATCH,), -1e+30, jnp.float32)
    start_total = jnp.zeros((BATCH,), jnp.float32)
    (peak, total), row_lse = lax.scan(first, (start_peak, start_total), image_blocks)
    col_lse = peak + jnp.log(total)
    columns = jnp.arange(BATCH, dtype=jnp.int32)

    def second(carry, item):
        text_acc, loss_acc, scale_acc = carry
        piece, lse_rows, number = item
        logits = scale * jnp.dot(piece, text_low.T, preferred_element_type=jnp.float32)
        rows = number * block + jnp.arange(block, dtype=jnp.int32)
        onehot = (rows[:, None] == columns[None, :]).astype(jnp.float32)
        delta = (jnp.exp(logits - lse_rows[:, None]) - onehot + (jnp.exp(logits - col_lse[None, :]) - onehot)) / (2.0 * BATCH)
        delta_low = delta.astype(jnp.bfloat16)
        image_grad = scale * jnp.dot(delta_low, text_low, preferred_element_type=jnp.float32)
        text_acc = text_acc + scale * jnp.dot(delta_low.T, piece, preferred_element_type=jnp.float32)
        loss_acc = loss_acc + jnp.sum(onehot * (lse_rows[:, None] + col_lse[None, :] - 2.0 * logits))
        scale_acc = scale_acc + jnp.sum(delta * logits)
        return ((text_acc, loss_acc, scale_acc), image_grad)
    numbers = jnp.arange(count, dtype=jnp.int32)
    start = (jnp.zeros((BATCH, E), jnp.float32), jnp.zeros((), jnp.float32), jnp.zeros((), jnp.float32))
    (text_grad, loss_sum, scale_sum), image_grad = lax.scan(second, start, (image_blocks, row_lse, numbers))
    image_grad = image_grad.reshape(BATCH, E)
    grad_images = image_inv * (image_grad - image_unit * lax.optimization_barrier(jnp.sum(image_unit * image_grad, axis=1, keepdims=True)))
    grad_texts = text_inv * (text_grad - text_unit * lax.optimization_barrier(jnp.sum(text_unit * text_grad, axis=1, keepdims=True)))
    return (grad_images, grad_texts, loss_sum / (2.0 * BATCH), scale_sum)
```

```python
import math

import jax
import jax.numpy as jnp
from jax import lax
from jax.experimental import pallas as pl
from jax.experimental.pallas import tpu as pltpu
from jax.sharding import PartitionSpec as P

EPS = 1e-06
LOG2E = math.log2(math.e)
LN2 = math.log(2.0)
MESH = pl.DeviceIdType.MESH
N = 4
R = 128
H = R // 2
E = 768
IMAGES = N * N * R
TEXTS = 2 * N * R
PAIRS = IMAGES // (2 * R)


def unit_rows(values):
    full = values.astype(jnp.float32)
    inverse = lax.rsqrt(jnp.sum(full * full, axis=1, keepdims=True) + EPS)
    return full * inverse, inverse


def lse2(values):
    peak = values[0]
    for v in values[1:]:
        peak = jnp.maximum(peak, v)
    total = jnp.exp2(values[0] - peak)
    for v in values[1:]:
        total = total + jnp.exp2(v - peak)
    return peak + jnp.log(total) * LOG2E


def project(values, grad):
    unit, inverse = unit_rows(values)
    return inverse * (grad - unit * jnp.sum(unit * grad, axis=1, keepdims=True))


def kernel(
    img_ref, txt_ref, scale_ref, gi_ref, gt_ref, loss_ref, gs_ref,
    img, txt, logit, delta, stage, own0, own1, a0, a1, sb0, sb1, b0, b1,
    tst, c0, sd, dd, rowl, rowy, rowz, coll, colc, colx, sums,
    ga_s, gb_s, g_r, tx_s, tc_s, t_r, ry_s, ry_r, rz_s, rz_r, cc_s, cc_r, cx_s, cx_r,
    pa_s, pa0_r, pa1_r, pb_s, pb_r, qc_s, qc_r, qx_s, qx_r, su_s, su_r,
):
    row, col = lax.axis_index("row"), lax.axis_index("col")
    x, c = row // 2, row % 2
    y, z = col // N, col % N
    sib = (row + 1 - 2 * c, col)

    def at_x(v):
        return (v * 2 + c, col)

    def at_y(v):
        return (row, v * N + z)

    def at_z(v):
        return (row, y * N + v)

    def turn(v, d):
        return lax.rem(v + d, N)

    def send(src, dst, ssem, rsem, dev):
        return pltpu.make_async_remote_copy(
            src_ref=src, dst_ref=dst, send_sem=ssem, recv_sem=rsem, device_id=dev, device_id_type=MESH
        )

    barrier = pltpu.get_barrier_semaphore()
    for d in range(1, N):
        for dev in (at_x(turn(x, d)), at_y(turn(y, d)), at_z(turn(z, d))):
            pl.semaphore_signal(barrier, inc=1, device_id=dev, device_id_type=MESH)
    pl.semaphore_signal(barrier, inc=1, device_id=sib, device_id_type=MESH)

    def block(k):
        return pl.ds(pl.multiple_of(k * R, R), R)

    def half(k, h):
        return pl.ds(pl.multiple_of(k * R + h * H, H), H)

    mine = c * N + x
    img[block(col), :] = unit_rows(img_ref[...])[0].astype(jnp.bfloat16)
    txt[block(mine), :] = unit_rows(txt_ref[...])[0].astype(jnp.bfloat16)
    scale = jnp.exp(jnp.full((1, 1), scale_ref[0], jnp.float32))
    scale2 = scale * LOG2E
    pl.semaphore_wait(barrier, 3 * (N - 1) + 1)

    def image_copy(k, h, ssem, dev):
        view = img.at[half(k, h), :]
        return send(view, view, ssem, g_r.at[k, h], dev)

    def text_copy(slot, ssem, dev):
        view = txt.at[block(slot), :]
        return send(view, view, ssem, t_r.at[slot], dev)

    first = []
    for d in range(1, N):
        first.append(image_copy(col, 0, ga_s.at[0, d], at_y(turn(y, d))))
        first.append(image_copy(col, 1, ga_s.at[1, d], at_z(turn(z, d))))
        first.append(text_copy(mine, tx_s.at[d], at_x(turn(x, d))))
    first.append(text_copy(mine, tc_s.at[0], sib))
    for d in range(1, N):
        first.append(image_copy(col, 0, gb_s.at[0, 0, d], at_z(turn(z, d))))
        first.append(image_copy(col, 1, gb_s.at[1, 0, d], at_y(turn(y, d))))
    for copy in first:
        copy.start()
    for d in (1, 3, 2):
        ky = turn(y, d) * N + z
        image_copy(ky, 0, ga_s.at[0, d], at_y(y)).wait_recv()
        for e in range(1, N):
            copy = image_copy(ky, 0, gb_s.at[0, d, e], at_z(turn(z, e)))
            copy.start()
            first.append(copy)
        kz = y * N + turn(z, d)
        image_copy(kz, 1, ga_s.at[1, d], at_z(z)).wait_recv()
        for e in range(1, N):
            copy = image_copy(kz, 1, gb_s.at[1, d, e], at_y(turn(y, e)))
            copy.start()
            first.append(copy)
        slot = c * N + turn(x, d)
        text_copy(slot, tx_s.at[d], sib).wait_recv()
        copy = text_copy(slot, tc_s.at[d], sib)
        copy.start()
        first.append(copy)
    for d in range(N):
        text_copy((1 - c) * N + turn(x, d), tc_s.at[d], sib).wait_recv()

    def tile_step(i, carry):
        p = lax.rem(col // 2 + i, PAIRS)
        for b in range(2):
            k = 2 * p + b

            @pl.when(k % N != z)
            def _():
                image_copy(k, 0, ga_s.at[0, 0], sib).wait_recv()

            @pl.when(k // N != y)
            def _():
                image_copy(k, 1, ga_s.at[0, 0], sib).wait_recv()

        rows = pl.ds(pl.multiple_of(p * 2 * R, 2 * R), 2 * R)
        l = scale2 * lax.dot_general(
            img[rows, :], txt[...], (((1,), (1,)), ((), ())), preferred_element_type=jnp.float32
        )
        logit[rows, :] = l
        rmax = jnp.max(l, axis=1, keepdims=True)
        cmax = jnp.max(l, axis=0, keepdims=True)
        rsum = jnp.sum(jnp.exp2(l - rmax), axis=1, keepdims=True)
        csum = jnp.sum(jnp.exp2(l - cmax), axis=0, keepdims=True)
        rlse = rmax + jnp.log(rsum) * LOG2E
        rowl[p] = jnp.broadcast_to(rlse, (2 * R, R)).T[:1, :]
        coll[p] = cmax + jnp.log(csum) * LOG2E
        return carry

    lax.fori_loop(0, PAIRS, tile_step, 0)

    rowy[y] = rowl[...]
    rowc = []
    for d in range(1, N):
        copy = send(rowy.at[y], rowy.at[y], ry_s.at[d], ry_r.at[y], at_y(turn(y, d)))
        copy.start()
        rowc.append(copy)
    colc[c] = lse2([coll[p] for p in range(PAIRS)])
    copy = send(colc.at[c], colc.at[c], cc_s.at[0], cc_r.at[c], sib)
    copy.start()
    rowc.append(copy)
    send(colc.at[1 - c], colc.at[1 - c], cc_s.at[0], cc_r.at[1 - c], sib).wait_recv()
    colx[x] = lse2([colc[0], colc[1]])
    for d in range(1, N):
        copy = send(colx.at[x], colx.at[x], cx_s.at[d], cx_r.at[x], at_x(turn(x, d)))
        copy.start()
        rowc.append(copy)
    for d in range(1, N):
        t = turn(y, d)
        send(rowy.at[t], rowy.at[t], ry_s.at[d], ry_r.at[t], sib).wait_recv()
    rowz[z] = lse2([rowy[v] for v in range(N)])
    for d in range(1, N):
        copy = send(rowz.at[z], rowz.at[z], rz_s.at[d], rz_r.at[z], at_z(turn(z, d)))
        copy.start()
        rowc.append(copy)
    for d in range(1, N):
        t = turn(x, d)
        send(colx.at[t], colx.at[t], cx_s.at[d], cx_r.at[t], sib).wait_recv()
    clse = lse2([colx[v] for v in range(N)])
    for d in range(1, N):
        t = turn(z, d)
        send(rowz.at[t], rowz.at[t], rz_s.at[d], rz_r.at[t], sib).wait_recv()
    rowl[...] = lse2([rowz[v] for v in range(N)])
    coll[0] = clse

    lane = lax.broadcasted_iota(jnp.int32, (8, R), 1)
    eye = lax.broadcasted_iota(jnp.int32, (R, R), 0) == lax.broadcasted_iota(jnp.int32, (R, R), 1)

    def a0_copy(k, dev):
        ky, kz = k // N, k % N
        return send(stage.at[half(k, 0), :], a0.at[y, kz], pa_s.at[k, 0], pa0_r.at[y, kz], (row, ky * N + z))

    def a1_copy(k, dev):
        ky, kz = k // N, k % N
        return send(stage.at[half(k, 1), :], a1.at[z, ky], pa_s.at[k, 1], pa1_r.at[z, ky], (row, y * N + kz))

    sums[0, c] = jnp.zeros((8, R), jnp.float32)

    def grad_step(i, total):
        p = lax.rem(2 * y + 2 + i, PAIRS)
        rows = pl.ds(pl.multiple_of(p * 2 * R, 2 * R), 2 * R)
        l = logit[rows, :]
        rcol = jnp.broadcast_to(rowl[p], (R, 2 * R)).T[:, :1]
        d = jnp.exp2(l - rcol) + jnp.exp2(l - coll[0])
        total = total + jnp.sum(d * l, axis=0, keepdims=True)
        delta[rows, :] = d.astype(jnp.bfloat16)
        for b in range(2):
            k = 2 * p + b
            j = row * (N * N) + k - col * (2 * N)

            @pl.when(jnp.logical_and(j >= 0, j < 2 * N))
            def _():
                cols = block((j % 2) * N + j // 2)
                sub = logit[block(k), cols]
                one = eye.astype(jnp.float32)
                rc = jnp.broadcast_to(rowl[p][:, b * R : (b + 1) * R], (R, R)).T[:, :1]
                cc = coll[0, :, cols]
                fixed = (jnp.exp2(sub - rc) - one) + (jnp.exp2(sub - cc) - one)
                delta[block(k), cols] = fixed.astype(jnp.bfloat16)
                lossp = jnp.sum(jnp.where(eye, rc + cc - 2.0 * sub, 0.0), axis=0, keepdims=True)
                lossp = jnp.sum(lossp, axis=1, keepdims=True)
                diag = jnp.sum(jnp.where(eye, -2.0 * sub, 0.0), axis=0, keepdims=True)
                diag = jnp.sum(diag, axis=1, keepdims=True)
                sums[0, c] = sums[0, c] + jnp.where(lane == 0, lossp, jnp.where(lane == 1, diag, 0.0))

        part = jnp.dot(delta[rows, :], txt[...], preferred_element_type=jnp.float32)
        stage[rows, :] = part.astype(jnp.bfloat16)
        for b in range(2):
            k = 2 * p + b
            ky, kz = k // N, k % N

            @pl.when(ky != y)
            def _():
                a0_copy(k, None).start()

            @pl.when(ky == y)
            def _():
                own0[kz] = part[b * R : b * R + H, :]

            @pl.when(kz != z)
            def _():
                a1_copy(k, None).start()

            @pl.when(kz == z)
            def _():
                own1[ky] = part[b * R + H : (b + 1) * R, :]

        return total

    total = lax.fori_loop(0, PAIRS, grad_step, jnp.zeros((1, TEXTS), jnp.float32))
    total = jnp.sum(total, axis=1, keepdims=True)
    sums[0, c] = sums[0, c] + jnp.where(lane == 1, total, 0.0)

    def sum_copies(level, at, where, count):
        return [
            send(sums.at[level, at], sums.at[level, at], su_s.at[level, d], su_r.at[level, at], where(d))
            for d in range(1, count)
        ]

    def sum_wait(level, at):
        send(sums.at[level, at], sums.at[level, at], su_s.at[level, 0], su_r.at[level, at], sib).wait_recv()

    copies = sum_copies(0, c, lambda d: sib, 2)
    copies[0].start()
    rowc += copies

    other = pl.ds(pl.multiple_of((1 - c) * N * R, N * R), N * R)
    ours = pl.ds(pl.multiple_of(c * N * R, N * R), N * R)
    tst[...] = lax.dot_general(
        delta[:, other], img[...], (((0,), (0,)), ((), ())), preferred_element_type=jnp.float32
    ).astype(jnp.bfloat16)
    for v in range(N):
        copy = send(tst.at[pl.ds(v * R, R), :], c0.at[v], qc_s.at[v], qc_r.at[v], sib)
        copy.start()
        rowc.append(copy)
    sum_wait(0, 1 - c)
    sums[1, x] = sums[0, 0] + sums[0, 1]
    copies = sum_copies(1, x, lambda d: at_x(turn(x, d)), N)
    for copy in copies:
        copy.start()
    rowc += copies
    qown = lax.dot_general(
        delta[:, ours], img[...], (((0,), (0,)), ((), ())), preferred_element_type=jnp.float32
    )
    for v in range(N):
        send(c0.at[v], c0.at[v], qc_s.at[v], qc_r.at[v], sib).wait_recv()
        sd[v] = qown[v * R : (v + 1) * R, :] + c0[v].astype(jnp.float32)
        dd[N + v] = sd[v].astype(jnp.bfloat16)
    for d in range(1, N):
        t = turn(x, d)
        copy = send(dd.at[N + t], dd.at[x], qx_s.at[d], qx_r.at[x], at_x(t))
        copy.start()
        rowc.append(copy)
    for d in range(1, N):
        sum_wait(1, turn(x, d))
    sums[2, y] = sums[1, 0] + sums[1, 1] + sums[1, 2] + sums[1, 3]
    copies = sum_copies(2, y, lambda d: at_y(turn(y, d)), N)
    for copy in copies:
        copy.start()
    rowc += copies

    for d in (1, 2, 3, 0):
        t = turn(z, d)
        acc = own0[t]
        for e in range(1, N):
            s = turn(y, e)
            send(a0.at[s, t], a0.at[s, t], pa_s.at[0, 0], pa0_r.at[s, t], sib).wait_recv()
            acc = acc + a0[s, t].astype(jnp.float32)
        own0[t] = acc
        if d:
            sb0[d] = acc.astype(jnp.bfloat16)
            copy = send(sb0.at[d], b0.at[z], pb_s.at[0, d], pb_r.at[0, z], at_z(t))
            copy.start()
            rowc.append(copy)
        t = turn(y, d)
        acc = own1[t]
        for e in range(1, N):
            s = turn(z, e)
            send(a1.at[s, t], a1.at[s, t], pa_s.at[0, 0], pa1_r.at[s, t], sib).wait_recv()
            acc = acc + a1[s, t].astype(jnp.float32)
        own1[t] = acc
        if d:
            sb1[d] = acc.astype(jnp.bfloat16)
            copy = send(sb1.at[d], b1.at[y], pb_s.at[1, d], pb_r.at[1, y], at_y(t))
            copy.start()
            rowc.append(copy)
    for d in range(1, N):
        sum_wait(2, turn(y, d))
    sums[3, z] = sums[2, 0] + sums[2, 1] + sums[2, 2] + sums[2, 3]
    copies = sum_copies(3, z, lambda d: at_z(turn(z, d)), N)
    for copy in copies:
        copy.start()
    rowc += copies

    factor = scale * (1.0 / (2.0 * TEXTS * N * N))
    acc = sd[x]
    for d in range(1, N):
        t = turn(x, d)
        send(dd.at[t], dd.at[t], qx_s.at[d], qx_r.at[t], sib).wait_recv()
        acc = acc + dd[t].astype(jnp.float32)
    gt_ref[...] = project(txt_ref[...], factor * acc)
    acc = own0[z]
    for d in range(1, N):
        t = turn(z, d)
        send(b0.at[t], b0.at[t], pb_s.at[0, d], pb_r.at[0, t], sib).wait_recv()
        acc = acc + b0[t].astype(jnp.float32)
    gi_ref[:H, :] = project(img_ref[:H, :], factor * acc)
    acc = own1[y]
    for d in range(1, N):
        t = turn(y, d)
        send(b1.at[t], b1.at[t], pb_s.at[1, d], pb_r.at[1, t], sib).wait_recv()
        acc = acc + b1[t].astype(jnp.float32)
    gi_ref[H:, :] = project(img_ref[H:, :], factor * acc)
    for d in range(1, N):
        sum_wait(3, turn(z, d))
    whole = (sums[3, 0] + sums[3, 1] + sums[3, 2] + sums[3, 3]) * (LN2 / (2.0 * TEXTS * N * N))
    top = lax.broadcasted_iota(jnp.int32, (8, R), 0) == 0
    loss_ref[0] = jnp.sum(jnp.where(jnp.logical_and(top, lane == 0), whole, 0.0))
    gs_ref[0] = jnp.sum(jnp.where(jnp.logical_and(top, lane == 1), whole, 0.0))

    for copy in first + rowc:
        copy.wait_send()

    def drain(k, carry):
        @pl.when(k // N != y)
        def _():
            a0_copy(k, None).wait_send()

        @pl.when(k % N != z)
        def _():
            a1_copy(k, None).wait_send()

        return carry

    lax.fori_loop(0, N * N, drain, 0)


def local(images, texts, log_scale):
    f32, bf16 = jnp.float32, jnp.bfloat16
    dma = pltpu.SemaphoreType.DMA
    vmem = pl.BlockSpec(memory_space=pltpu.VMEM)
    smem = pl.BlockSpec(memory_space=pltpu.SMEM)
    gi, gt, loss, gs = pl.pallas_call(
        kernel,
        out_shape=(
            jax.ShapeDtypeStruct((R, E), f32),
            jax.ShapeDtypeStruct((R, E), f32),
            jax.ShapeDtypeStruct((1,), f32),
            jax.ShapeDtypeStruct((1,), f32),
        ),
        in_specs=[vmem, vmem, smem],
        out_specs=(vmem, vmem, smem, smem),
        scratch_shapes=[
            pltpu.VMEM((IMAGES, E), bf16),
            pltpu.VMEM((TEXTS, E), bf16),
            pltpu.VMEM((IMAGES, TEXTS), f32),
            pltpu.VMEM((IMAGES, TEXTS), bf16),
            pltpu.VMEM((IMAGES, E), bf16),
            pltpu.VMEM((N, H, E), f32),
            pltpu.VMEM((N, H, E), f32),
            pltpu.VMEM((N, N, H, E), bf16),
            pltpu.VMEM((N, N, H, E), bf16),
            pltpu.VMEM((N, H, E), bf16),
            pltpu.VMEM((N, H, E), bf16),
            pltpu.VMEM((N, H, E), bf16),
            pltpu.VMEM((N, H, E), bf16),
            pltpu.VMEM((N * R, E), bf16),
            pltpu.VMEM((N, R, E), bf16),
            pltpu.VMEM((N, R, E), f32),
            pltpu.VMEM((2 * N, R, E), bf16),
            pltpu.VMEM((PAIRS, 1, 2 * R), f32),
            pltpu.VMEM((N, PAIRS, 1, 2 * R), f32),
            pltpu.VMEM((N, PAIRS, 1, 2 * R), f32),
            pltpu.VMEM((PAIRS, 1, TEXTS), f32),
            pltpu.VMEM((2, 1, TEXTS), f32),
            pltpu.VMEM((N, 1, TEXTS), f32),
            pltpu.VMEM((4, N, 8, R), f32),
            dma((2, N)),
            dma((2, N, N)),
            dma((N * N, 2)),
            dma((N,)),
            dma((N,)),
            dma((2 * N,)),
            dma((N,)), dma((N,)), dma((N,)), dma((N,)),
            dma((1,)), dma((2,)), dma((N,)), dma((N,)),
            dma((N * N, 2)), dma((N, N)), dma((N, N)),
            dma((2, N)), dma((2, N)),
            dma((N,)), dma((N,)), dma((N,)), dma((N,)),
            dma((4, N)), dma((4, N)),
        ],
        compiler_params=pltpu.CompilerParams(
            collective_id=0, has_side_effects=True, vmem_limit_bytes=56 * 1024 * 1024
        ),
    )(images, texts, log_scale.reshape(1))
    return gi, gt, loss.reshape(()), gs.reshape(())


def solution(mesh):
    placed = (P(("row", "col"), None), P(("col", "row"), None), P())
    return jax.shard_map(
        local,
        mesh=mesh,
        in_specs=placed,
        out_specs=(P(("row", "col"), None), P(("col", "row"), None), P(), P()),
        check_vma=False,
    )
```

```python
import math

import jax
import jax.numpy as jnp
from jax import lax
from jax.experimental import pallas as pl
from jax.experimental.pallas import tpu as pltpu
from jax.sharding import PartitionSpec as P

EPS = 1e-06
LOG2E = math.log2(math.e)
LN2 = math.log(2.0)
MESH = pl.DeviceIdType.MESH
N = 4
R = 128
H = R // 2
E = 768
IMAGES = N * N * R
TEXTS = 2 * N * R
PAIRS = IMAGES // (2 * R)


def unit_rows(values):
    full = values.astype(jnp.float32)
    inverse = lax.rsqrt(jnp.sum(full * full, axis=1, keepdims=True) + EPS)
    return full * inverse, inverse


def lse2(values):
    peak = values[0]
    for v in values[1:]:
        peak = jnp.maximum(peak, v)
    total = jnp.exp2(values[0] - peak)
    for v in values[1:]:
        total = total + jnp.exp2(v - peak)
    return peak + jnp.log(total) * LOG2E


def project(values, grad):
    unit, inverse = unit_rows(values)
    return inverse * (grad - unit * jnp.sum(unit * grad, axis=1, keepdims=True))


def kernel(
    img_ref, txt_ref, scale_ref, gi_ref, gt_ref, loss_ref, gs_ref,
    img, txt, logit, delta, stage_s, stage_c, stage_i, stage_t,
    own0, own1, a0, a1, sb, b0, b1,
    rowl, rowp, rowx, coll, colp, colz, sums,
    g_s, g_r, t_r, rp_r, rx_r, cp_r, cz_r, qc_s, qc_r, pa0_s, pa1_s, pa0_r, pa1_r, pb0_r, pb1_r, su_r,
):
    row, col = lax.axis_index("row"), lax.axis_index("col")
    x, c = row // 2, row % 2
    y, z = col // N, col % N
    yb, yo = y % 2, y // 2
    yi = y + 1 - 2 * yb
    yt = N - 1 - y
    sib = (row + 1 - 2 * c, col)
    by_i = (row, yi * N + z)
    by_t = (row, yt * N + z)
    by_is = (row + 1 - 2 * c, yi * N + z)

    def at_x(v):
        return (v * 2 + c, col)

    def at_z(v):
        return (row, y * N + v)

    def turn(v, d):
        return lax.rem(v + d, N)

    def send(src, dst, ssem, rsem, dev):
        return pltpu.make_async_remote_copy(
            src_ref=src, dst_ref=dst, send_sem=ssem, recv_sem=rsem, device_id=dev, device_id_type=MESH
        )

    started = []

    def go(src, dst, rsem, dev):
        copy = send(src, dst, g_s.at[len(started)], rsem, dev)
        copy.start()
        started.append(copy)

    def take(dst, rsem):
        send(dst, dst, g_s.at[0], rsem, sib).wait_recv()

    barrier = pltpu.get_barrier_semaphore()
    peers = [by_i, by_t, by_is, sib]
    for d in range(1, N):
        peers += [at_x(turn(x, d)), at_z(turn(z, d))]
    for dev in peers:
        pl.semaphore_signal(barrier, inc=1, device_id=dev, device_id_type=MESH)

    def block(k):
        return pl.ds(pl.multiple_of(k * R, R), R)

    def pair(p):
        return pl.ds(pl.multiple_of(p * 2 * R, 2 * R), 2 * R)

    def half(k, h):
        return pl.ds(pl.multiple_of(k * R + h * H, H), H)

    def islot(cc, b, xx):
        return cc * 2 * N + b * N + xx

    def tslot(o, zz):
        return o * N + zz

    imine, tmine = islot(c, yb, x), tslot(yo, z)
    img[block(imine), :] = unit_rows(img_ref[...])[0].astype(jnp.bfloat16)
    txt[block(tmine), :] = unit_rows(txt_ref[...])[0].astype(jnp.bfloat16)
    scale = jnp.exp(jnp.full((1, 1), scale_ref[0], jnp.float32))
    scale2 = scale * LOG2E
    pl.semaphore_wait(barrier, len(peers))

    def iview(k, h):
        return img.at[half(k, h), :]

    def tview(k, h):
        return txt.at[half(k, h), :]

    def igo(k, h, dev):
        go(iview(k, h), iview(k, h), g_r.at[k, h], dev)

    def tgo(k, h, dev):
        go(tview(k, h), tview(k, h), t_r.at[k, h], dev)

    def itake(k, h):
        take(iview(k, h), g_r.at[k, h])

    def ttake(k, h):
        take(tview(k, h), t_r.at[k, h])

    igo(imine, 0, by_i)
    tgo(tmine, 0, by_t)
    for h in (1, 0):
        for d in range(1, N):
            igo(imine, h, at_x(turn(x, d)))
            tgo(tmine, h, at_z(turn(z, d)))
    igo(imine, 1, by_i)
    tgo(tmine, 1, by_t)
    for h in range(2):
        igo(imine, h, sib)
    k = islot(c, 1 - yb, x)
    itake(k, 0)
    for d in range(1, N):
        igo(k, 0, at_x(turn(x, d)))
    t = tslot(1 - yo, z)
    ttake(t, 0)
    for d in range(1, N):
        tgo(t, 0, at_z(turn(z, d)))
    igo(k, 0, sib)
    for d in (1, 3, 2):
        k = islot(c, yb, turn(x, d))
        itake(k, 1)
        igo(k, 1, by_i)
        igo(k, 1, sib)
        t = tslot(yo, turn(z, d))
        ttake(t, 1)
        tgo(t, 1, by_t)
    for d in (1, 3, 2):
        k = islot(c, yb, turn(x, d))
        itake(k, 0)
        igo(k, 0, sib)
    for d in (1, 3, 2):
        ttake(tslot(yo, turn(z, d)), 0)

    def tile(p, o):
        cols = pl.ds(pl.multiple_of(o * N * R, N * R), N * R)
        l = scale2 * lax.dot_general(
            img[pair(p), :], txt[cols, :], (((1,), (1,)), ((), ())), preferred_element_type=jnp.float32
        )
        logit[pair(p), cols] = l
        rmax = jnp.max(l, axis=1, keepdims=True)
        cmax = jnp.max(l, axis=0, keepdims=True)
        rsum = jnp.sum(jnp.exp2(l - rmax), axis=1, keepdims=True)
        csum = jnp.sum(jnp.exp2(l - cmax), axis=0, keepdims=True)
        rlse = rmax + jnp.log(rsum) * LOG2E
        rowl[o, pl.ds(p, 1), :] = jnp.broadcast_to(rlse, (2 * R, R)).T[:1, :]
        coll[p, :, cols] = cmax + jnp.log(csum) * LOG2E

    def tiles(b, o, fresh):
        def step(i, carry):
            cc = lax.rem(c + i // 2, 2)
            p = cc * N + b * 2 + i % 2
            if fresh:

                @pl.when(i >= 2)
                def _():
                    for j in range(2):
                        for h in range(2):
                            itake(2 * p + j, h)

            tile(p, o)
            return carry

        lax.fori_loop(0, N, step, 0)

    tiles(yb, yo, True)
    k = islot(c, 1 - yb, x)
    itake(k, 1)
    igo(k, 1, sib)
    for h in (1, 0):
        for d in (1, 3, 2):
            k = islot(c, 1 - yb, turn(x, d))
            itake(k, h)
            igo(k, h, sib)
    for d in range(N):
        t = tslot(1 - yo, turn(z, d))
        ttake(t, 1)
        if d:
            ttake(t, 0)
    tiles(yb, 1 - yo, False)
    tiles(1 - yb, yo, True)
    tiles(1 - yb, 1 - yo, False)

    me = 2 * yb + c
    rowp[me] = lse2([rowl[0], rowl[1]])
    for dev in (by_i, by_is, sib):
        go(rowp.at[me], rowp.at[me], rp_r.at[me], dev)
    colp[yo] = lse2([coll[p] for p in range(PAIRS)])
    go(colp.at[yo], colp.at[yo], cp_r.at[yo], by_t)
    for v in (2 * yb + 1 - c, 2 - 2 * yb + c, 3 - 2 * yb - c):
        take(rowp.at[v], rp_r.at[v])
    rowx[x] = lse2([rowp[v] for v in range(N)])
    for d in range(1, N):
        go(rowx.at[x], rowx.at[x], rx_r.at[x], at_x(turn(x, d)))
    take(colp.at[1 - yo], cp_r.at[1 - yo])
    colz[z] = lse2([colp[0], colp[1]])
    for d in range(1, N):
        go(colz.at[z], colz.at[z], cz_r.at[z], at_z(turn(z, d)))
    for d in range(1, N):
        v = turn(x, d)
        take(rowx.at[v], rx_r.at[v])
    rowl[0] = lse2([rowx[v] for v in range(N)])
    for d in range(1, N):
        v = turn(z, d)
        take(colz.at[v], cz_r.at[v])
    coll[0] = lse2([colz[v] for v in range(N)])

    lane = lax.broadcasted_iota(jnp.int32, (8, R), 1)
    eye = lax.broadcasted_iota(jnp.int32, (R, R), 0) == lax.broadcasted_iota(jnp.int32, (R, R), 1)
    sums[0, c] = jnp.zeros((8, R), jnp.float32)

    def delta_step(p, total):
        l = logit[pair(p), :]
        lse = rowl[0, pl.ds(p, 1), :]
        rcol = jnp.broadcast_to(lse, (R, 2 * R)).T[:, :1]
        d = jnp.exp2(l - rcol) + jnp.exp2(l - coll[0])
        total = total + jnp.sum(d * l, axis=0, keepdims=True)
        delta[pair(p), :] = d.astype(jnp.bfloat16)
        for b in range(2):
            k = 2 * p + b
            irow = k % N * 2 + k // (2 * N)
            icol = (yo * 2 + k // N % 2) * N + z
            trow, tcol = icol % (2 * N), irow * 2 + icol // (2 * N)
            ty = tcol // N

            @pl.when(jnp.logical_and(trow == row, jnp.logical_or(ty == y, ty == yt)))
            def _():
                cols = block(tslot(ty // 2, tcol % N))
                sub = logit[block(k), cols]
                one = eye.astype(jnp.float32)
                rc = jnp.broadcast_to(lse[:, b * R : (b + 1) * R], (R, R)).T[:, :1]
                cc = coll[0, :, cols]
                fixed = (jnp.exp2(sub - rc) - one) + (jnp.exp2(sub - cc) - one)
                delta[block(k), cols] = fixed.astype(jnp.bfloat16)
                lossp = jnp.sum(jnp.where(eye, rc + cc - 2.0 * sub, 0.0), axis=0, keepdims=True)
                lossp = jnp.sum(lossp, axis=1, keepdims=True)
                diag = jnp.sum(jnp.where(eye, -2.0 * sub, 0.0), axis=0, keepdims=True)
                diag = jnp.sum(diag, axis=1, keepdims=True)
                sums[0, c] = sums[0, c] + jnp.where(lane == 0, lossp, jnp.where(lane == 1, diag, 0.0))

        return total

    total = lax.fori_loop(0, PAIRS, delta_step, jnp.zeros((1, TEXTS), jnp.float32))
    total = jnp.sum(total, axis=1, keepdims=True)
    sums[0, c] = sums[0, c] + jnp.where(lane == 1, total, 0.0)

    def sum_go(level, at, devs):
        for dev in devs:
            go(sums.at[level, at], sums.at[level, at], su_r.at[level, at], dev)

    def sum_take(level, at):
        take(sums.at[level, at], su_r.at[level, at])

    sum_go(0, c, [sib])

    ring_me, pair_me = (x, z), (yb, yo)
    ring_at, partner = (at_x, at_z), (by_i, by_t)
    stages = (stage_i, stage_t)

    def h0_copy(m, g, b, v):
        return send(
            stages[m].at[half(g, 0), :], a0.at[m, ring_me[m], b], pa0_s.at[m, g],
            pa0_r.at[m, ring_me[m], b], ring_at[m](v),
        )

    def h1_copy(m, g, v):
        return send(stages[m].at[half(g, 1), :], a1.at[m, v], pa1_s.at[m, g], pa1_r.at[m, v], partner[m])

    def emit(m, j, part):
        stages[m][pair(j), :] = part.astype(jnp.bfloat16)
        b = j // 2
        for i in range(2):
            g = 2 * j + i
            v = g % N

            @pl.when(v != ring_me[m])
            def _():
                h0_copy(m, g, b, v).start()

            @pl.when(v == ring_me[m])
            def _():
                own0[m, b] = part[i * R : i * R + H, :]

            @pl.when(b != pair_me[m])
            def _():
                h1_copy(m, g, v).start()

            @pl.when(b == pair_me[m])
            def _():
                own1[m, v] = part[i * R + H : (i + 1) * R, :]

    def sib_copy(j):
        return send(stage_s.at[pair(j), :], stage_c.at[pair(j), :], qc_s.at[j], qc_r.at[j], sib)

    def order(m, i):
        return lax.rem(pair_me[m] + 1 + i // 2, 2) * 2 + lax.rem(ring_me[m] // 2 + 1 + i, 2)

    def grad_step(i, carry):
        j = order(0, i)
        part = jnp.dot(delta[pair((1 - c) * N + j), :], txt[...], preferred_element_type=jnp.float32)
        stage_s[pair(j), :] = part.astype(jnp.bfloat16)
        sib_copy(j).start()
        q = order(1, i)
        emit(
            1, q,
            lax.dot_general(
                delta[:, pair(q)], img[...], (((0,), (0,)), ((), ())), preferred_element_type=jnp.float32
            ),
        )
        part = jnp.dot(delta[pair(c * N + j), :], txt[...], preferred_element_type=jnp.float32)
        sib_copy(j).wait_recv()
        emit(0, j, part + stage_c[pair(j), :].astype(jnp.float32))
        return carry

    lax.fori_loop(0, N, grad_step, 0)
    sum_take(0, 1 - c)
    sums[1, x] = sums[0, 0] + sums[0, 1]
    sum_go(1, x, [at_x(turn(x, d)) for d in range(1, N)])

    def h0_sum(m, b):
        acc = own0[m, b]
        for d in range(1, N):
            s = turn(ring_me[m], d)
            take(a0.at[m, s, b], pa0_r.at[m, s, b])
            acc = acc + a0[m, s, b].astype(jnp.float32)
        return acc

    def h1_sum(m, v):
        take(a1.at[m, v], pa1_r.at[m, v])
        return own1[m, v] + a1[m, v].astype(jnp.float32)

    for m in range(2):
        sb[m, 0] = h0_sum(m, 1 - pair_me[m]).astype(jnp.bfloat16)
        go(sb.at[m, 0], b0.at[m], pb0_r.at[m], partner[m])
    for d in range(1, N):
        for m in range(2):
            v = turn(ring_me[m], d)
            sb[m, d] = h1_sum(m, v).astype(jnp.bfloat16)
            go(sb.at[m, d], b1.at[m, ring_me[m]], pb1_r.at[m, ring_me[m]], ring_at[m](v))
    for d in range(1, N):
        sum_take(1, turn(x, d))
    sums[2, yb] = sums[1, 0] + sums[1, 1] + sums[1, 2] + sums[1, 3]
    sum_go(2, yb, [by_i])
    for m in range(2):
        own0[m, 0] = h0_sum(m, pair_me[m])
        own1[m, 0] = h1_sum(m, ring_me[m])
    sum_take(2, 1 - yb)
    sums[3, yo] = sums[2, 0] + sums[2, 1]
    sum_go(3, yo, [by_t])

    factor = scale * (1.0 / (2.0 * TEXTS * N * N))
    sources, results = (img_ref, txt_ref), (gi_ref, gt_ref)
    for m in range(2):
        take(b0.at[m], pb0_r.at[m])
        acc = own0[m, 0] + b0[m].astype(jnp.float32)
        results[m][:H, :] = project(sources[m][:H, :], factor * acc)
    sum_take(3, 1 - yo)
    sums[4, z] = sums[3, 0] + sums[3, 1]
    sum_go(4, z, [at_z(turn(z, d)) for d in range(1, N)])
    for m in range(2):
        acc = own1[m, 0]
        for d in range(1, N):
            s = turn(ring_me[m], d)
            take(b1.at[m, s], pb1_r.at[m, s])
            acc = acc + b1[m, s].astype(jnp.float32)
        results[m][H:, :] = project(sources[m][H:, :], factor * acc)
    for d in range(1, N):
        sum_take(4, turn(z, d))
    whole = (sums[4, 0] + sums[4, 1] + sums[4, 2] + sums[4, 3]) * (LN2 / (2.0 * TEXTS * N * N))
    top = lax.broadcasted_iota(jnp.int32, (8, R), 0) == 0
    loss_ref[0] = jnp.sum(jnp.where(jnp.logical_and(top, lane == 0), whole, 0.0))
    gs_ref[0] = jnp.sum(jnp.where(jnp.logical_and(top, lane == 1), whole, 0.0))

    for copy in started:
        copy.wait_send()

    def drain(g, carry):
        v, b = g % N, g // N
        for m in range(2):

            @pl.when(v != ring_me[m])
            def _():
                h0_copy(m, g, b, v).wait_send()

            @pl.when(b != pair_me[m])
            def _():
                h1_copy(m, g, v).wait_send()

        return carry

    lax.fori_loop(0, 2 * N, drain, 0)
    for j in range(N):
        sib_copy(j).wait_send()


def local(images, texts, log_scale):
    f32, bf16 = jnp.float32, jnp.bfloat16
    dma = pltpu.SemaphoreType.DMA
    vmem = pl.BlockSpec(memory_space=pltpu.VMEM)
    smem = pl.BlockSpec(memory_space=pltpu.SMEM)
    gi, gt, loss, gs = pl.pallas_call(
        kernel,
        out_shape=(
            jax.ShapeDtypeStruct((R, E), f32),
            jax.ShapeDtypeStruct((R, E), f32),
            jax.ShapeDtypeStruct((1,), f32),
            jax.ShapeDtypeStruct((1,), f32),
        ),
        in_specs=[vmem, vmem, smem],
        out_specs=(vmem, vmem, smem, smem),
        scratch_shapes=[
            pltpu.VMEM((IMAGES, E), bf16),
            pltpu.VMEM((TEXTS, E), bf16),
            pltpu.VMEM((IMAGES, TEXTS), f32),
            pltpu.VMEM((IMAGES, TEXTS), bf16),
            pltpu.VMEM((TEXTS, E), bf16),
            pltpu.VMEM((TEXTS, E), bf16),
            pltpu.VMEM((TEXTS, E), bf16),
            pltpu.VMEM((TEXTS, E), bf16),
            pltpu.VMEM((2, 2, H, E), f32),
            pltpu.VMEM((2, N, H, E), f32),
            pltpu.VMEM((2, N, 2, H, E), bf16),
            pltpu.VMEM((2, N, H, E), bf16),
            pltpu.VMEM((2, N, H, E), bf16),
            pltpu.VMEM((2, H, E), bf16),
            pltpu.VMEM((2, N, H, E), bf16),
            pltpu.VMEM((2, PAIRS, 2 * R), f32),
            pltpu.VMEM((N, PAIRS, 2 * R), f32),
            pltpu.VMEM((N, PAIRS, 2 * R), f32),
            pltpu.VMEM((PAIRS, 1, TEXTS), f32),
            pltpu.VMEM((2, 1, TEXTS), f32),
            pltpu.VMEM((N, 1, TEXTS), f32),
            pltpu.VMEM((5, N, 8, R), f32),
            dma((96,)),
            dma((N * N, 2)),
            dma((2 * N, 2)),
            dma((N,)), dma((N,)), dma((2,)), dma((N,)),
            dma((N,)), dma((N,)),
            dma((2, 2 * N)), dma((2, 2 * N)),
            dma((2, N, 2)), dma((2, N)),
            dma((2,)), dma((2, N)),
            dma((5, N)),
        ],
        compiler_params=pltpu.CompilerParams(
            collective_id=0, has_side_effects=True, vmem_limit_bytes=56 * 1024 * 1024
        ),
    )(images, texts, log_scale.reshape(1))
    return gi, gt, loss.reshape(()), gs.reshape(())


def solution(mesh):
    placed = (P(("row", "col"), None), P(("col", "row"), None), P())
    return jax.shard_map(
        local,
        mesh=mesh,
        in_specs=placed,
        out_specs=(P(("row", "col"), None), P(("col", "row"), None), P(), P()),
        check_vma=False,
    )
```

```python
import math

import jax
import jax.numpy as jnp
from jax import lax
from jax.experimental import pallas as pl
from jax.experimental.pallas import tpu as pltpu
from jax.sharding import PartitionSpec as P

EPS = 1e-06
LOG2E = math.log2(math.e)
LN2 = math.log(2.0)
MESH = pl.DeviceIdType.MESH
N = 4
R = 128
H = R // 2
E = 768
IMAGES = N * N * R
TEXTS = 2 * N * R
PAIRS = IMAGES // (2 * R)


def unit_rows(values):
    full = values.astype(jnp.float32)
    inverse = lax.rsqrt(jnp.sum(full * full, axis=1, keepdims=True) + EPS)
    return full * inverse, inverse


def lse2(values):
    peak = values[0]
    for v in values[1:]:
        peak = jnp.maximum(peak, v)
    total = jnp.exp2(values[0] - peak)
    for v in values[1:]:
        total = total + jnp.exp2(v - peak)
    return peak + jnp.log(total) * LOG2E


def project(values, grad):
    unit, inverse = unit_rows(values)
    return inverse * (grad - unit * jnp.sum(unit * grad, axis=1, keepdims=True))


def kernel(
    img_ref, txt_ref, scale_ref, gi_ref, gt_ref, loss_ref, gs_ref,
    img, txt, logit, delta, stage_s, stage_c, stage_i, stage_t,
    own0, own1, a0, a1, sb, b0, b1,
    rowl, rowp, rowx, coll, colz, sums,
    g_s, g_r, t_r, rp_r, rx_r, cz_r, qc_s, qc_r, pa0_s, pa1_s, pa0_r, pa1_r, pb0_r, pb1_r, su_r,
):
    row, col = lax.axis_index("row"), lax.axis_index("col")
    x, c = row // 2, row % 2
    y, z = col // N, col % N
    yb, yo = y % 2, y // 2
    yi = y + 1 - 2 * yb
    yt = N - 1 - y
    sib = (row + 1 - 2 * c, col)
    by_i = (row, yi * N + z)
    by_t = (row, yt * N + z)
    def at_x(v):
        return (v * 2 + c, col)

    def at_z(v):
        return (row, y * N + v)

    def turn(v, d):
        return lax.rem(v + d, N)

    same_i = [at_x(turn(x, d)) for d in range(1, N)]
    same_i += [(turn(x, d) * 2 + c, yi * N + z) for d in (1, 3, 2)] + [by_i]
    same_t = [at_z(turn(z, d)) for d in range(1, N)]
    same_t += [(row, yt * N + turn(z, d)) for d in (1, 3, 2)] + [by_t]

    def send(src, dst, ssem, rsem, dev):
        return pltpu.make_async_remote_copy(
            src_ref=src, dst_ref=dst, send_sem=ssem, recv_sem=rsem, device_id=dev, device_id_type=MESH
        )

    started = []

    def go(src, dst, rsem, dev):
        copy = send(src, dst, g_s.at[len(started)], rsem, dev)
        copy.start()
        started.append(copy)

    def take(dst, rsem):
        send(dst, dst, g_s.at[0], rsem, sib).wait_recv()

    barrier = pltpu.get_barrier_semaphore()
    peers = same_i + same_t + [sib]
    for dev in peers:
        pl.semaphore_signal(barrier, inc=1, device_id=dev, device_id_type=MESH)

    def block(k):
        return pl.ds(pl.multiple_of(k * R, R), R)

    def pair(p):
        return pl.ds(pl.multiple_of(p * 2 * R, 2 * R), 2 * R)

    def half(k, h):
        return pl.ds(pl.multiple_of(k * R + h * H, H), H)

    def islot(cc, b, xx):
        return cc * 2 * N + b * N + xx

    def tslot(o, zz):
        return o * N + zz

    imine, tmine = islot(c, yb, x), tslot(yo, z)
    img[block(imine), :] = unit_rows(img_ref[...])[0].astype(jnp.bfloat16)
    txt[block(tmine), :] = unit_rows(txt_ref[...])[0].astype(jnp.bfloat16)
    scale = jnp.exp(jnp.full((1, 1), scale_ref[0], jnp.float32))
    scale2 = scale * LOG2E
    pl.semaphore_wait(barrier, len(peers))

    def iview(k, h):
        return img.at[half(k, h), :]

    def tview(k, h):
        return txt.at[half(k, h), :]

    def igo(k, h, dev):
        go(iview(k, h), iview(k, h), g_r.at[k, h], dev)

    def tgo(k, h, dev):
        go(tview(k, h), tview(k, h), t_r.at[k, h], dev)

    def itake(k, h):
        take(iview(k, h), g_r.at[k, h])

    def ttake(k, h):
        take(tview(k, h), t_r.at[k, h])

    igo(imine, 0, by_i)
    tgo(tmine, 0, by_t)
    for h in (1, 0):
        for d in range(1, N):
            igo(imine, h, at_x(turn(x, d)))
            tgo(tmine, h, at_z(turn(z, d)))
    igo(imine, 1, by_i)
    tgo(tmine, 1, by_t)
    for h in range(2):
        igo(imine, h, sib)
    k = islot(c, 1 - yb, x)
    itake(k, 0)
    for d in range(1, N):
        igo(k, 0, at_x(turn(x, d)))
    t = tslot(1 - yo, z)
    ttake(t, 0)
    for d in range(1, N):
        tgo(t, 0, at_z(turn(z, d)))
    igo(k, 0, sib)
    for d in (1, 3, 2):
        k = islot(c, yb, turn(x, d))
        itake(k, 1)
        igo(k, 1, by_i)
        igo(k, 1, sib)
        t = tslot(yo, turn(z, d))
        ttake(t, 1)
        tgo(t, 1, by_t)
    for d in (1, 3, 2):
        k = islot(c, yb, turn(x, d))
        itake(k, 0)
        igo(k, 0, sib)
    for d in (1, 3, 2):
        ttake(tslot(yo, turn(z, d)), 0)

    def tile(q, o):
        rows = pl.ds(pl.multiple_of(q * N * R, N * R), N * R)
        cols = pl.ds(pl.multiple_of(o * N * R, N * R), N * R)
        l = scale2 * lax.dot_general(
            img[rows, :], txt[cols, :], (((1,), (1,)), ((), ())), preferred_element_type=jnp.float32
        )
        logit[rows, cols] = l
        rmax = jnp.max(l, axis=1, keepdims=True)
        cmax = jnp.max(l, axis=0, keepdims=True)
        rsum = jnp.sum(jnp.exp2(l - rmax), axis=1, keepdims=True)
        csum = jnp.sum(jnp.exp2(l - cmax), axis=0, keepdims=True)
        rlse = rmax + jnp.log(rsum) * LOG2E
        line = jnp.broadcast_to(rlse, (N * R, R)).T[:1, :]
        for i in range(2):
            rowl[o, pl.ds(2 * q + i, 1), :] = line[:, i * 2 * R : (i + 1) * 2 * R]
        coll[q, :, cols] = cmax + jnp.log(csum) * LOG2E

    def sib_blocks(b):
        for v in range(N):
            for h in range(2):
                itake(islot(1 - c, b, v), h)

    def tile_step(i, carry):
        @pl.when(i == 1)
        def _():
            sib_blocks(yb)

        @pl.when(i == 5)
        def _():
            sib_blocks(1 - yb)

        tile(lax.rem(c + i, 2) * 2 + lax.rem(yb + i // 4, 2), lax.rem(yo + i // 2, 2))
        return carry

    lax.fori_loop(0, 2, tile_step, 0)
    k = islot(c, 1 - yb, x)
    itake(k, 1)
    igo(k, 1, sib)
    for h in (1, 0):
        for d in (1, 3, 2):
            k = islot(c, 1 - yb, turn(x, d))
            itake(k, h)
            igo(k, h, sib)
    for d in range(N):
        t = tslot(1 - yo, turn(z, d))
        ttake(t, 1)
        if d:
            ttake(t, 0)
    lax.fori_loop(2, 2 * N, tile_step, 0)

    rowp[c] = lse2([rowl[0], rowl[1]])
    go(rowp.at[c], rowp.at[c], rp_r.at[c], sib)
    ime, tme = yb * N + x, yo * N + z
    colz[tme] = lse2([coll[q] for q in range(N)])
    for dev in same_t:
        go(colz.at[tme], colz.at[tme], cz_r.at[tme], dev)
    take(rowp.at[1 - c], rp_r.at[1 - c])
    rowx[ime] = lse2([rowp[0], rowp[1]])
    for dev in same_i:
        go(rowx.at[ime], rowx.at[ime], rx_r.at[ime], dev)

    def others(b, v):
        return [b * N + turn(v, d) for d in range(1, N)] + [(1 - b) * N + turn(v, d) for d in range(N)]

    for t in others(yo, z):
        take(colz.at[t], cz_r.at[t])
    coll[0] = lse2([colz[v] for v in range(2 * N)])
    for t in others(yb, x):
        take(rowx.at[t], rx_r.at[t])
    rowl[0] = lse2([rowx[v] for v in range(2 * N)])

    lane = lax.broadcasted_iota(jnp.int32, (8, R), 1)

    def meets(k):
        irow = k % N * 2 + k // (2 * N)
        icol = (yo * 2 + k // N % 2) * N + z
        trow, tcol = icol % (2 * N), irow * 2 + icol // (2 * N)
        ty = tcol // N
        here = jnp.logical_and(trow == row, jnp.logical_or(ty == y, ty == yt))
        return here, tslot(ty // 2, tcol % N)

    def delta_part(p, total):
        l = logit[pair(p), :]
        rcol = jnp.broadcast_to(rowl[0, pl.ds(p, 1), :], (R, 2 * R)).T[:, :1]
        target = lax.broadcasted_iota(jnp.int32, (2 * R, 1), 0)
        offs = []
        for i in range(2):
            here, slot = meets(2 * p + i)
            offs.append(jnp.where(here, (slot - i) * R, -4 * TEXTS))
        target = target + jnp.where(target < R, offs[0], offs[1])
        twice = jnp.where(lax.broadcasted_iota(jnp.int32, (2 * R, TEXTS), 1) == target, 2.0, 0.0)
        d = jnp.exp2(l - rcol) + jnp.exp2(l - coll[0]) - twice
        total = total + jnp.sum(d * l, axis=0, keepdims=True)
        low = d.astype(jnp.bfloat16)
        delta[pair(p), :] = low
        return jnp.dot(low, txt[...], preferred_element_type=jnp.float32), total

    def sum_go(level, at, devs):
        for dev in devs:
            go(sums.at[level, at], sums.at[level, at], su_r.at[level, at], dev)

    def sum_take(level, at):
        take(sums.at[level, at], su_r.at[level, at])

    ring_me, pair_me = (x, z), (yb, yo)
    ring_at, partner = (at_x, at_z), (by_i, by_t)
    stages = (stage_i, stage_t)

    def h0_copy(m, g, b, v):
        return send(
            stages[m].at[half(g, 0), :], a0.at[m, ring_me[m], b], pa0_s.at[m, g],
            pa0_r.at[m, ring_me[m], b], ring_at[m](v),
        )

    def h1_copy(m, g, v):
        return send(stages[m].at[half(g, 1), :], a1.at[m, v], pa1_s.at[m, g], pa1_r.at[m, v], partner[m])

    def emit(m, j, part):
        stages[m][pair(j), :] = part.astype(jnp.bfloat16)
        b = j // 2
        for i in range(2):
            g = 2 * j + i
            v = g % N

            @pl.when(v != ring_me[m])
            def _():
                h0_copy(m, g, b, v).start()

            @pl.when(v == ring_me[m])
            def _():
                own0[m, b] = part[i * R : i * R + H, :]

            @pl.when(b != pair_me[m])
            def _():
                h1_copy(m, g, v).start()

            @pl.when(b == pair_me[m])
            def _():
                own1[m, v] = part[i * R + H : (i + 1) * R, :]

    def sib_copy(j):
        return send(stage_s.at[pair(j), :], stage_c.at[pair(j), :], qc_s.at[j], qc_r.at[j], sib)

    def order(m, i):
        return lax.rem(pair_me[m] + 1 + i // 2, 2) * 2 + lax.rem(ring_me[m] // 2 + 1 + i, 2)

    def image_step(i, total):
        for u in range(2):
            j = order(0, 2 * i + u)
            part, total = delta_part((1 - c) * N + j, total)
            stage_s[pair(j), :] = part.astype(jnp.bfloat16)
            sib_copy(j).start()
        for u in range(2):
            j = order(0, 2 * i + u)
            part, total = delta_part(c * N + j, total)
            sib_copy(j).wait_recv()
            emit(0, j, part + stage_c[pair(j), :].astype(jnp.float32))
        return total

    total = lax.fori_loop(0, 2, image_step, jnp.zeros((1, TEXTS), jnp.float32))

    def text_step(i, carry):
        q = order(1, i)
        emit(
            1, q,
            lax.dot_general(
                delta[:, pair(q)], img[...], (((0,), (0,)), ((), ())), preferred_element_type=jnp.float32
            ),
        )
        return carry

    lax.fori_loop(0, N, text_step, 0)

    sums[0, c] = jnp.where(lane == 1, jnp.sum(total, axis=1, keepdims=True), jnp.zeros((8, R), jnp.float32))
    eye = lax.broadcasted_iota(jnp.int32, (R, R), 0) == lax.broadcasted_iota(jnp.int32, (R, R), 1)

    def loss_step(k, carry):
        here, slot = meets(k)

        @pl.when(here)
        def _():
            cols = block(slot)
            both = rowl[0, pl.ds(k // 2, 1), :]
            rl = jnp.where(k % 2 == 0, both[:, :R], both[:, R:])
            pairs = jnp.sum(jnp.where(eye, logit[block(k), cols], 0.0), axis=0, keepdims=True)
            part = jnp.sum(rl + coll[0, :, cols] - 2.0 * pairs, axis=1, keepdims=True)
            sums[0, c] = sums[0, c] + jnp.where(lane == 0, part, 0.0)

        return carry

    lax.fori_loop(0, N * N, loss_step, 0)
    sum_go(0, c, [sib])

    def h0_sum(m, b):
        acc = own0[m, b]
        for d in range(1, N):
            s = turn(ring_me[m], d)
            take(a0.at[m, s, b], pa0_r.at[m, s, b])
            acc = acc + a0[m, s, b].astype(jnp.float32)
        return acc

    def h1_sum(m, v):
        take(a1.at[m, v], pa1_r.at[m, v])
        return own1[m, v] + a1[m, v].astype(jnp.float32)

    def second(m):
        sb[m, 0] = h0_sum(m, 1 - pair_me[m]).astype(jnp.bfloat16)
        go(sb.at[m, 0], b0.at[m], pb0_r.at[m], partner[m])
        for d in (2, 1, 3):
            v = turn(ring_me[m], d)
            sb[m, d] = h1_sum(m, v).astype(jnp.bfloat16)
            go(sb.at[m, d], b1.at[m, ring_me[m]], pb1_r.at[m, ring_me[m]], ring_at[m](v))
        own0[m, 0] = h0_sum(m, pair_me[m])
        own1[m, 0] = h1_sum(m, ring_me[m])

    second(0)
    sum_take(0, 1 - c)
    sums[1, ime] = sums[0, 0] + sums[0, 1]
    sum_go(1, ime, same_i)
    second(1)
    for t in others(yb, x):
        sum_take(1, t)
    acc = sums[1, 0]
    for v in range(1, 2 * N):
        acc = acc + sums[1, v]
    sums[2, tme] = acc
    sum_go(2, tme, same_t)

    factor = scale * (1.0 / (2.0 * TEXTS * N * N))
    sources, results = (img_ref, txt_ref), (gi_ref, gt_ref)
    for m in range(2):
        take(b0.at[m], pb0_r.at[m])
        acc = own0[m, 0] + b0[m].astype(jnp.float32)
        results[m][:H, :] = project(sources[m][:H, :], factor * acc)
        acc = own1[m, 0]
        for d in range(1, N):
            s = turn(ring_me[m], d)
            take(b1.at[m, s], pb1_r.at[m, s])
            acc = acc + b1[m, s].astype(jnp.float32)
        results[m][H:, :] = project(sources[m][H:, :], factor * acc)
    for t in others(yo, z):
        sum_take(2, t)
    whole = sums[2, 0]
    for v in range(1, 2 * N):
        whole = whole + sums[2, v]
    whole = whole * (LN2 / (2.0 * TEXTS * N * N))
    top = lax.broadcasted_iota(jnp.int32, (8, R), 0) == 0
    loss_ref[0] = jnp.sum(jnp.where(jnp.logical_and(top, lane == 0), whole, 0.0))
    gs_ref[0] = jnp.sum(jnp.where(jnp.logical_and(top, lane == 1), whole, 0.0))

    for copy in started:
        copy.wait_send()

    def drain(g, carry):
        v, b = g % N, g // N
        for m in range(2):

            @pl.when(v != ring_me[m])
            def _():
                h0_copy(m, g, b, v).wait_send()

            @pl.when(b != pair_me[m])
            def _():
                h1_copy(m, g, v).wait_send()

        return carry

    lax.fori_loop(0, 2 * N, drain, 0)
    for j in range(N):
        sib_copy(j).wait_send()


def local(images, texts, log_scale):
    f32, bf16 = jnp.float32, jnp.bfloat16
    dma = pltpu.SemaphoreType.DMA
    vmem = pl.BlockSpec(memory_space=pltpu.VMEM)
    smem = pl.BlockSpec(memory_space=pltpu.SMEM)
    gi, gt, loss, gs = pl.pallas_call(
        kernel,
        out_shape=(
            jax.ShapeDtypeStruct((R, E), f32),
            jax.ShapeDtypeStruct((R, E), f32),
            jax.ShapeDtypeStruct((1,), f32),
            jax.ShapeDtypeStruct((1,), f32),
        ),
        in_specs=[vmem, vmem, smem],
        out_specs=(vmem, vmem, smem, smem),
        scratch_shapes=[
            pltpu.VMEM((IMAGES, E), bf16),
            pltpu.VMEM((TEXTS, E), bf16),
            pltpu.VMEM((IMAGES, TEXTS), f32),
            pltpu.VMEM((IMAGES, TEXTS), bf16),
            pltpu.VMEM((TEXTS, E), bf16),
            pltpu.VMEM((TEXTS, E), bf16),
            pltpu.VMEM((TEXTS, E), bf16),
            pltpu.VMEM((TEXTS, E), bf16),
            pltpu.VMEM((2, 2, H, E), f32),
            pltpu.VMEM((2, N, H, E), f32),
            pltpu.VMEM((2, N, 2, H, E), bf16),
            pltpu.VMEM((2, N, H, E), bf16),
            pltpu.VMEM((2, N, H, E), bf16),
            pltpu.VMEM((2, H, E), bf16),
            pltpu.VMEM((2, N, H, E), bf16),
            pltpu.VMEM((2, PAIRS, 2 * R), f32),
            pltpu.VMEM((2, PAIRS, 2 * R), f32),
            pltpu.VMEM((2 * N, PAIRS, 2 * R), f32),
            pltpu.VMEM((N, 1, TEXTS), f32),
            pltpu.VMEM((2 * N, 1, TEXTS), f32),
            pltpu.VMEM((3, 2 * N, 8, R), f32),
            dma((96,)),
            dma((N * N, 2)),
            dma((2 * N, 2)),
            dma((2,)), dma((2 * N,)), dma((2 * N,)),
            dma((N,)), dma((N,)),
            dma((2, 2 * N)), dma((2, 2 * N)),
            dma((2, N, 2)), dma((2, N)),
            dma((2,)), dma((2, N)),
            dma((3, 2 * N)),
        ],
        compiler_params=pltpu.CompilerParams(
            collective_id=0, has_side_effects=True, vmem_limit_bytes=56 * 1024 * 1024
        ),
    )(images, texts, log_scale.reshape(1))
    return gi, gt, loss.reshape(()), gs.reshape(())


def solution(mesh):
    placed = (P(("row", "col"), None), P(("col", "row"), None), P())
    return jax.shard_map(
        local,
        mesh=mesh,
        in_specs=placed,
        out_specs=(P(("row", "col"), None), P(("col", "row"), None), P(), P()),
        check_vma=False,
    )
```

```python
import math

import jax
import jax.numpy as jnp
from jax import lax
from jax.experimental import pallas as pl
from jax.experimental.pallas import tpu as pltpu
from jax.sharding import PartitionSpec as P

EPS = 1e-06
LOG2E = math.log2(math.e)
LN2 = math.log(2.0)
MESH = pl.DeviceIdType.MESH
N = 4
R = 128
H = R // 2
E = 768
IMAGES = N * N * R
TEXTS = 2 * N * R
PAIRS = IMAGES // (2 * R)


def unit_rows(values):
    full = values.astype(jnp.float32)
    inverse = lax.rsqrt(jnp.sum(full * full, axis=1, keepdims=True) + EPS)
    return full * inverse, inverse


def lse2(values):
    peak = values[0]
    for v in values[1:]:
        peak = jnp.maximum(peak, v)
    total = jnp.exp2(values[0] - peak)
    for v in values[1:]:
        total = total + jnp.exp2(v - peak)
    return peak + jnp.log(total) * LOG2E


def project(values, grad):
    unit, inverse = unit_rows(values)
    return inverse * (grad - unit * jnp.sum(unit * grad, axis=1, keepdims=True))


def kernel(
    img_ref, txt_ref, scale_ref, gi_ref, gt_ref, loss_ref, gs_ref,
    img, txt, logit, delta, stage_s, stage_c, stage_i, stage_t,
    own0, own1, fin, a0, a1, sb, b0, b1,
    rowl, rowp, rowx, coll, colz, sums,
    g_s, g_r, t_r, rp_r, rx_r, cz_r, qc_s, qc_r, pa0_s, pa1_s, pa0_r, pa1_r, pb0_r, pb1_r, su_r,
):
    row, col = lax.axis_index("row"), lax.axis_index("col")
    x, c = row // 2, row % 2
    y, z = col // N, col % N
    yb, yo = y % 2, y // 2
    yi = y + 1 - 2 * yb
    yt = N - 1 - y
    sib = (row + 1 - 2 * c, col)
    by_i = (row, yi * N + z)
    by_t = (row, yt * N + z)
    def at_x(v):
        return (v * 2 + c, col)

    def at_z(v):
        return (row, y * N + v)

    def turn(v, d):
        return lax.rem(v + d, N)

    same_i = [at_x(turn(x, d)) for d in range(1, N)]
    same_i += [(turn(x, d) * 2 + c, yi * N + z) for d in (1, 3, 2)] + [by_i]
    same_t = [at_z(turn(z, d)) for d in range(1, N)]
    same_t += [(row, yt * N + turn(z, d)) for d in (1, 3, 2)] + [by_t]

    def send(src, dst, ssem, rsem, dev):
        return pltpu.make_async_remote_copy(
            src_ref=src, dst_ref=dst, send_sem=ssem, recv_sem=rsem, device_id=dev, device_id_type=MESH
        )

    started = []

    def go(src, dst, rsem, dev):
        copy = send(src, dst, g_s.at[len(started)], rsem, dev)
        copy.start()
        started.append(copy)

    def take(dst, rsem):
        send(dst, dst, g_s.at[0], rsem, sib).wait_recv()

    barrier = pltpu.get_barrier_semaphore()
    peers = same_i[: N - 1] + same_t[: N - 1] + [by_i, by_t, sib]
    for dev in peers:
        pl.semaphore_signal(barrier, inc=1, device_id=dev, device_id_type=MESH)

    def block(k):
        return pl.ds(pl.multiple_of(k * R, R), R)

    def pair(p):
        return pl.ds(pl.multiple_of(p * 2 * R, 2 * R), 2 * R)

    def half(k, h):
        return pl.ds(pl.multiple_of(k * R + h * H, H), H)

    def islot(cc, b, xx):
        return cc * 2 * N + b * N + xx

    def tslot(o, zz):
        return o * N + zz

    imine, tmine = islot(c, yb, x), tslot(yo, z)
    img[block(imine), :] = unit_rows(img_ref[...])[0].astype(jnp.bfloat16)
    txt[block(tmine), :] = unit_rows(txt_ref[...])[0].astype(jnp.bfloat16)
    scale = jnp.exp(jnp.full((1, 1), scale_ref[0], jnp.float32))
    scale2 = scale * LOG2E
    pl.semaphore_wait(barrier, len(peers))

    def iview(k, h):
        return img.at[half(k, h), :]

    def tview(k, h):
        return txt.at[half(k, h), :]

    def igo(k, h, dev):
        go(iview(k, h), iview(k, h), g_r.at[k, h], dev)

    def tgo(k, h, dev):
        go(tview(k, h), tview(k, h), t_r.at[k, h], dev)

    def itake(k, h):
        take(iview(k, h), g_r.at[k, h])

    def ttake(k, h):
        take(tview(k, h), t_r.at[k, h])

    igo(imine, 0, by_i)
    tgo(tmine, 0, by_t)
    for h in (1, 0):
        for d in range(1, N):
            igo(imine, h, at_x(turn(x, d)))
            tgo(tmine, h, at_z(turn(z, d)))
    igo(imine, 1, by_i)
    tgo(tmine, 1, by_t)
    for h in range(2):
        igo(imine, h, sib)
    k = islot(c, 1 - yb, x)
    itake(k, 0)
    for d in range(1, N):
        igo(k, 0, at_x(turn(x, d)))
    t = tslot(1 - yo, z)
    ttake(t, 0)
    for d in range(1, N):
        tgo(t, 0, at_z(turn(z, d)))
    igo(k, 0, sib)
    for d in (1, 3, 2):
        k = islot(c, yb, turn(x, d))
        itake(k, 1)
        igo(k, 1, by_i)
        igo(k, 1, sib)
        t = tslot(yo, turn(z, d))
        ttake(t, 1)
        tgo(t, 1, by_t)
    for d in (1, 3, 2):
        k = islot(c, yb, turn(x, d))
        itake(k, 0)
        igo(k, 0, sib)
    for d in (1, 3, 2):
        ttake(tslot(yo, turn(z, d)), 0)

    def tile(q, o):
        rows = pl.ds(pl.multiple_of(q * N * R, N * R), N * R)
        cols = pl.ds(pl.multiple_of(o * N * R, N * R), N * R)
        l = scale2 * lax.dot_general(
            img[rows, :], txt[cols, :], (((1,), (1,)), ((), ())), preferred_element_type=jnp.float32
        )
        logit[rows, cols] = l
        rmax = jnp.max(l, axis=1, keepdims=True)
        cmax = jnp.max(l, axis=0, keepdims=True)
        rsum = jnp.sum(jnp.exp2(l - rmax), axis=1, keepdims=True)
        csum = jnp.sum(jnp.exp2(l - cmax), axis=0, keepdims=True)
        rlse = rmax + jnp.log(rsum) * LOG2E
        line = jnp.broadcast_to(rlse, (N * R, R)).T[:1, :]
        for i in range(2):
            rowl[o, pl.ds(2 * q + i, 1), :] = line[:, i * 2 * R : (i + 1) * 2 * R]
        coll[q, :, cols] = cmax + jnp.log(csum) * LOG2E

    def sib_blocks(b):
        for v in range(N):
            for h in range(2):
                itake(islot(1 - c, b, v), h)

    def tile_step(i, carry):
        @pl.when(i == 1)
        def _():
            sib_blocks(yb)

        @pl.when(i == 5)
        def _():
            sib_blocks(1 - yb)

        tile(lax.rem(c + i, 2) * 2 + lax.rem(yb + i // 4, 2), lax.rem(yo + i // 2, 2))
        return carry

    lax.fori_loop(0, 2, tile_step, 0)
    k = islot(c, 1 - yb, x)
    itake(k, 1)
    igo(k, 1, sib)
    for h in (1, 0):
        for d in (1, 3, 2):
            k = islot(c, 1 - yb, turn(x, d))
            itake(k, h)
            igo(k, h, sib)
    for d in range(N):
        t = tslot(1 - yo, turn(z, d))
        ttake(t, 1)
        if d:
            ttake(t, 0)
    lax.fori_loop(2, 2 * N, tile_step, 0)

    rowp[c] = lse2([rowl[0], rowl[1]])
    go(rowp.at[c], rowp.at[c], rp_r.at[c], sib)
    ime, tme = yb * N + x, yo * N + z
    colz[tme] = lse2([coll[q] for q in range(N)])
    for dev in same_t:
        go(colz.at[tme], colz.at[tme], cz_r.at[tme], dev)
    take(rowp.at[1 - c], rp_r.at[1 - c])
    rowx[ime] = lse2([rowp[0], rowp[1]])
    for dev in same_i:
        go(rowx.at[ime], rowx.at[ime], rx_r.at[ime], dev)

    def others(b, v):
        return [b * N + turn(v, d) for d in range(1, N)] + [(1 - b) * N + turn(v, d) for d in range(N)]

    for t in others(yo, z):
        take(colz.at[t], cz_r.at[t])
    coll[0] = lse2([colz[v] for v in range(2 * N)])
    for t in others(yb, x):
        take(rowx.at[t], rx_r.at[t])
    rowl[0] = lse2([rowx[v] for v in range(2 * N)])

    lane = lax.broadcasted_iota(jnp.int32, (8, R), 1)

    def meets(k):
        irow = k % N * 2 + k // (2 * N)
        icol = (yo * 2 + k // N % 2) * N + z
        trow, tcol = icol % (2 * N), irow * 2 + icol // (2 * N)
        ty = tcol // N
        here = jnp.logical_and(trow == row, jnp.logical_or(ty == y, ty == yt))
        return here, tslot(ty // 2, tcol % N)

    def delta_part(p, total):
        l = logit[pair(p), :]
        rcol = jnp.broadcast_to(rowl[0, pl.ds(p, 1), :], (R, 2 * R)).T[:, :1]
        target = lax.broadcasted_iota(jnp.int32, (2 * R, 1), 0)
        offs = []
        for i in range(2):
            here, slot = meets(2 * p + i)
            offs.append(jnp.where(here, (slot - i) * R, -4 * TEXTS))
        target = target + jnp.where(target < R, offs[0], offs[1])
        twice = jnp.where(lax.broadcasted_iota(jnp.int32, (2 * R, TEXTS), 1) == target, 2.0, 0.0)
        d = jnp.exp2(l - rcol) + jnp.exp2(l - coll[0]) - twice
        total = total + jnp.sum(d * l, axis=0, keepdims=True)
        low = d.astype(jnp.bfloat16)
        delta[pair(p), :] = low
        return jnp.dot(low, txt[...], preferred_element_type=jnp.float32), total

    def sum_go(level, at, devs):
        for dev in devs:
            go(sums.at[level, at], sums.at[level, at], su_r.at[level, at], dev)

    def sum_take(level, at):
        take(sums.at[level, at], su_r.at[level, at])

    ring_me, pair_me = (x, z), (yb, yo)
    ring_at, partner = (at_x, at_z), (by_i, by_t)
    stages = (stage_i, stage_t)

    def h0_copy(m, g, b, v):
        return send(
            stages[m].at[half(g, 0), :], a0.at[m, ring_me[m], b], pa0_s.at[m, g],
            pa0_r.at[m, ring_me[m], b], ring_at[m](v),
        )

    def h1_copy(m, g, v):
        return send(stages[m].at[half(g, 1), :], a1.at[m, v], pa1_s.at[m, g], pa1_r.at[m, v], partner[m])

    def spot(m, i):
        b = pair_me[m] if i // 2 else 1 - pair_me[m]
        near = ring_me[m] // 2
        return b, near if i % 2 else 1 - near

    def order(m, i):
        b, half_ring = spot(m, i)
        return b * 2 + half_ring

    def twin(m):
        return ring_me[m] + 1 - ring_me[m] % 2 * 2

    def emit(m, i, part):
        b, half_ring = spot(m, i)
        stages[m][pair(order(m, i)), :] = part.astype(jnp.bfloat16)
        for t in range(2):
            v = 2 * half_ring + t
            if i % 2:
                own0[m, i // 2, t] = part[t * R : t * R + H, :]
            else:
                h0_copy(m, b * N + v, b, v).start()
            if i // 2:
                own1[m, v] = part[t * R + H : (t + 1) * R, :]
            else:
                h1_copy(m, b * N + v, v).start()
        if i % 2:
            h0_copy(m, b * N + twin(m), b, twin(m)).start()

    def sib_copy(j):
        return send(stage_s.at[pair(j), :], stage_c.at[pair(j), :], qc_s.at[j], qc_r.at[j], sib)

    def sib_step(i, total):
        js = [lax.rem(1 - yb + i, 2) * 2 + v for v in (1 - x // 2, x // 2)]
        for j in js:
            part, total = delta_part((1 - c) * N + j, total)
            stage_s[pair(j), :] = part.astype(jnp.bfloat16)
        for j in js:
            sib_copy(j).start()
        return total

    total = lax.fori_loop(0, 2, sib_step, jnp.zeros((1, TEXTS), jnp.float32))
    for i in (0, 2):
        parts = []
        for u in range(2):
            part, total = delta_part(c * N + order(0, i + u), total)
            parts.append(part)
        for u in range(2):
            j = order(0, i + u)
            sib_copy(j).wait_recv()
            emit(0, i + u, parts[u] + stage_c[pair(j), :].astype(jnp.float32))

    def text_part(i):
        return lax.dot_general(
            delta[:, pair(order(1, i))], img[...], (((0,), (0,)), ((), ())), preferred_element_type=jnp.float32
        )

    for i in (0, 2):
        parts = [text_part(i), text_part(i + 1)]
        for u in range(2):
            emit(1, i + u, parts[u])

    sums[0, c] = jnp.where(lane == 1, jnp.sum(total, axis=1, keepdims=True), jnp.zeros((8, R), jnp.float32))
    eye = lax.broadcasted_iota(jnp.int32, (R, R), 0) == lax.broadcasted_iota(jnp.int32, (R, R), 1)

    def loss_step(k, carry):
        here, slot = meets(k)

        @pl.when(here)
        def _():
            cols = block(slot)
            both = rowl[0, pl.ds(k // 2, 1), :]
            rl = jnp.where(k % 2 == 0, both[:, :R], both[:, R:])
            pairs = jnp.sum(jnp.where(eye, logit[block(k), cols], 0.0), axis=0, keepdims=True)
            part = jnp.sum(rl + coll[0, :, cols] - 2.0 * pairs, axis=1, keepdims=True)
            sums[0, c] = sums[0, c] + jnp.where(lane == 0, part, 0.0)

        return carry

    lax.fori_loop(0, N * N, loss_step, 0)
    sum_go(0, c, [sib])

    def h0_sum(m, i):
        b = pair_me[m] if i else 1 - pair_me[m]
        acc = own0[m, i, ring_me[m] % 2]
        for d in range(1, N):
            s = turn(ring_me[m], d)
            take(a0.at[m, s, b], pa0_r.at[m, s, b])
            acc = acc + a0[m, s, b].astype(jnp.float32)
        return acc

    def h1_sum(m, v):
        take(a1.at[m, v], pa1_r.at[m, v])
        return own1[m, v] + a1[m, v].astype(jnp.float32)

    def second0(m):
        sb[m, N] = h0_sum(m, 0).astype(jnp.bfloat16)
        go(sb.at[m, N], b0.at[m], pb0_r.at[m], partner[m])

    def second1(m, v):
        sb[m, v] = h1_sum(m, v).astype(jnp.bfloat16)
        go(sb.at[m, v], b1.at[m, ring_me[m]], pb1_r.at[m, ring_me[m]], ring_at[m](v))

    def far_blocks(m):
        v = 2 - ring_me[m] // 2 * 2
        return v, v + 1

    for v in far_blocks(0):
        second1(0, v)
    second0(0)
    sum_take(0, 1 - c)
    sums[1, ime] = sums[0, 0] + sums[0, 1]
    sum_go(1, ime, same_i)
    for v in far_blocks(1):
        second1(1, v)
    second1(0, twin(0))
    second0(1)
    second1(1, twin(1))
    for t in others(yb, x):
        sum_take(1, t)
    acc = sums[1, 0]
    for v in range(1, 2 * N):
        acc = acc + sums[1, v]
    sums[2, tme] = acc
    sum_go(2, tme, same_t)
    for m in range(2):
        fin[m, 0] = h0_sum(m, 1)
        fin[m, 1] = h1_sum(m, ring_me[m])

    factor = scale * (1.0 / (2.0 * TEXTS * N * N))
    sources, results = (img_ref, txt_ref), (gi_ref, gt_ref)
    for m in range(2):
        take(b0.at[m], pb0_r.at[m])
        acc = fin[m, 0] + b0[m].astype(jnp.float32)
        results[m][:H, :] = project(sources[m][:H, :], factor * acc)
        acc = fin[m, 1]
        for d in range(1, N):
            s = turn(ring_me[m], d)
            take(b1.at[m, s], pb1_r.at[m, s])
            acc = acc + b1[m, s].astype(jnp.float32)
        results[m][H:, :] = project(sources[m][H:, :], factor * acc)
    for t in others(yo, z):
        sum_take(2, t)
    whole = sums[2, 0]
    for v in range(1, 2 * N):
        whole = whole + sums[2, v]
    whole = whole * (LN2 / (2.0 * TEXTS * N * N))
    top = lax.broadcasted_iota(jnp.int32, (8, R), 0) == 0
    loss_ref[0] = jnp.sum(jnp.where(jnp.logical_and(top, lane == 0), whole, 0.0))
    gs_ref[0] = jnp.sum(jnp.where(jnp.logical_and(top, lane == 1), whole, 0.0))

    for copy in started:
        copy.wait_send()

    for m in range(2):
        for b in range(2):
            for d in range(1, N):
                v = turn(ring_me[m], d)
                h0_copy(m, b * N + v, b, v).wait_send()
        for v in range(N):
            h1_copy(m, (1 - pair_me[m]) * N + v, v).wait_send()
    for j in range(N):
        sib_copy(j).wait_send()


def local(images, texts, log_scale):
    f32, bf16 = jnp.float32, jnp.bfloat16
    dma = pltpu.SemaphoreType.DMA
    vmem = pl.BlockSpec(memory_space=pltpu.VMEM)
    smem = pl.BlockSpec(memory_space=pltpu.SMEM)
    gi, gt, loss, gs = pl.pallas_call(
        kernel,
        out_shape=(
            jax.ShapeDtypeStruct((R, E), f32),
            jax.ShapeDtypeStruct((R, E), f32),
            jax.ShapeDtypeStruct((1,), f32),
            jax.ShapeDtypeStruct((1,), f32),
        ),
        in_specs=[vmem, vmem, smem],
        out_specs=(vmem, vmem, smem, smem),
        scratch_shapes=[
            pltpu.VMEM((IMAGES, E), bf16),
            pltpu.VMEM((TEXTS, E), bf16),
            pltpu.VMEM((IMAGES, TEXTS), f32),
            pltpu.VMEM((IMAGES, TEXTS), bf16),
            pltpu.VMEM((TEXTS, E), bf16),
            pltpu.VMEM((TEXTS, E), bf16),
            pltpu.VMEM((TEXTS, E), bf16),
            pltpu.VMEM((TEXTS, E), bf16),
            pltpu.VMEM((2, 2, 2, H, E), f32),
            pltpu.VMEM((2, N, H, E), f32),
            pltpu.VMEM((2, 2, H, E), f32),
            pltpu.VMEM((2, N, 2, H, E), bf16),
            pltpu.VMEM((2, N, H, E), bf16),
            pltpu.VMEM((2, N + 1, H, E), bf16),
            pltpu.VMEM((2, H, E), bf16),
            pltpu.VMEM((2, N, H, E), bf16),
            pltpu.VMEM((2, PAIRS, 2 * R), f32),
            pltpu.VMEM((2, PAIRS, 2 * R), f32),
            pltpu.VMEM((2 * N, PAIRS, 2 * R), f32),
            pltpu.VMEM((N, 1, TEXTS), f32),
            pltpu.VMEM((2 * N, 1, TEXTS), f32),
            pltpu.VMEM((3, 2 * N, 8, R), f32),
            dma((96,)),
            dma((N * N, 2)),
            dma((2 * N, 2)),
            dma((2,)), dma((2 * N,)), dma((2 * N,)),
            dma((N,)), dma((N,)),
            dma((2, 2 * N)), dma((2, 2 * N)),
            dma((2, N, 2)), dma((2, N)),
            dma((2,)), dma((2, N)),
            dma((3, 2 * N)),
        ],
        compiler_params=pltpu.CompilerParams(
            collective_id=0, has_side_effects=True, vmem_limit_bytes=56 * 1024 * 1024
        ),
    )(images, texts, log_scale.reshape(1))
    return gi, gt, loss.reshape(()), gs.reshape(())


def solution(mesh):
    placed = (P(("row", "col"), None), P(("col", "row"), None), P())
    return jax.shard_map(
        local,
        mesh=mesh,
        in_specs=placed,
        out_specs=(P(("row", "col"), None), P(("col", "row"), None), P(), P()),
        check_vma=False,
    )
```

```python
import math

import jax
import jax.numpy as jnp
from jax import lax
from jax.experimental import pallas as pl
from jax.experimental.pallas import tpu as pltpu
from jax.sharding import PartitionSpec as P

EPS = 1e-06
LOG2E = math.log2(math.e)
LN2 = math.log(2.0)
MESH = pl.DeviceIdType.MESH
N = 4
R = 128
H = R // 2
E = 768
IMAGES = N * N * R
TEXTS = 2 * N * R
PAIRS = IMAGES // (2 * R)


def unit_rows(values):
    full = values.astype(jnp.float32)
    inverse = lax.rsqrt(jnp.sum(full * full, axis=1, keepdims=True) + EPS)
    return full * inverse, inverse


def lse2(values):
    peak = values[0]
    for v in values[1:]:
        peak = jnp.maximum(peak, v)
    total = jnp.exp2(values[0] - peak)
    for v in values[1:]:
        total = total + jnp.exp2(v - peak)
    return peak + jnp.log(total) * LOG2E


def project(values, grad):
    unit, inverse = unit_rows(values)
    return inverse * (grad - unit * jnp.sum(unit * grad, axis=1, keepdims=True))


def kernel(
    img_ref, txt_ref, scale_ref, gi_ref, gt_ref, loss_ref, gs_ref,
    img, txt, logit, delta, stage_s, stage_c, stage_i, stage_t,
    own0, own1, fin, a0, a1, sb, b0, b1,
    rowl, rowp, rowx, coll, colz, sums,
    g_s, g_r, t_r, rp_r, rx_r, cz_r, qc_s, qc_r, pa0_s, pa1_s, pa0_r, pa1_r, pb0_r, pb1_r, su_r,
):
    row, col = lax.axis_index("row"), lax.axis_index("col")
    x, c = row // 2, row % 2
    y, z = col // N, col % N
    yb, yo = y % 2, y // 2
    yi = y + 1 - 2 * yb
    yt = N - 1 - y
    sib = (row + 1 - 2 * c, col)
    by_i = (row, yi * N + z)
    by_t = (row, yt * N + z)
    def at_x(v):
        return (v * 2 + c, col)

    def at_z(v):
        return (row, y * N + v)

    def turn(v, d):
        return lax.rem(v + d, N)

    x_up, x_down, z_up, z_down = turn(x, 1), turn(x, 3), turn(z, 1), turn(z, 3)

    same_i = [at_x(turn(x, d)) for d in range(1, N)]
    same_i += [(turn(x, d) * 2 + c, yi * N + z) for d in (1, 3, 2)] + [by_i]
    same_t = [at_z(turn(z, d)) for d in range(1, N)]
    same_t += [(row, yt * N + turn(z, d)) for d in (1, 3, 2)] + [by_t]

    def send(src, dst, ssem, rsem, dev):
        return pltpu.make_async_remote_copy(
            src_ref=src, dst_ref=dst, send_sem=ssem, recv_sem=rsem, device_id=dev, device_id_type=MESH
        )

    started = []

    def go(src, dst, rsem, dev):
        copy = send(src, dst, g_s.at[len(started)], rsem, dev)
        copy.start()
        started.append(copy)

    def take(dst, rsem):
        send(dst, dst, g_s.at[0], rsem, sib).wait_recv()

    barrier = pltpu.get_barrier_semaphore()
    peers = [at_x(x_up), at_x(x_down), at_z(z_up), at_z(z_down), by_i, by_t, sib]
    for dev in peers:
        pl.semaphore_signal(barrier, inc=1, device_id=dev, device_id_type=MESH)

    def block(k):
        return pl.ds(pl.multiple_of(k * R, R), R)

    def pair(p):
        return pl.ds(pl.multiple_of(p * 2 * R, 2 * R), 2 * R)

    def half(k, h):
        return pl.ds(pl.multiple_of(k * R + h * H, H), H)

    def islot(cc, b, xx):
        return cc * 2 * N + b * N + xx

    def tslot(o, zz):
        return o * N + zz

    imine, tmine = islot(c, yb, x), tslot(yo, z)
    img[block(imine), :] = unit_rows(img_ref[...])[0].astype(jnp.bfloat16)
    txt[block(tmine), :] = unit_rows(txt_ref[...])[0].astype(jnp.bfloat16)
    scale = jnp.exp(jnp.full((1, 1), scale_ref[0], jnp.float32))
    scale2 = scale * LOG2E
    pl.semaphore_wait(barrier, len(peers))

    def iview(k, h):
        return img.at[half(k, h), :]

    def tview(k, h):
        return txt.at[half(k, h), :]

    def igo(k, h, dev):
        go(iview(k, h), iview(k, h), g_r.at[k, h], dev)

    def tgo(k, h, dev):
        go(tview(k, h), tview(k, h), t_r.at[k, h], dev)

    def itake(k, h):
        take(iview(k, h), g_r.at[k, h])

    def ttake(k, h):
        take(tview(k, h), t_r.at[k, h])

    igo(imine, 0, by_i)
    tgo(tmine, 0, by_t)
    for h in (1, 0):
        for v, w in ((x_up, z_up), (x_down, z_down)):
            igo(imine, h, at_x(v))
            tgo(tmine, h, at_z(w))
    igo(imine, 1, by_i)
    tgo(tmine, 1, by_t)
    for h in range(2):
        igo(imine, h, sib)

    def ipass(b, v, h, devs):
        k = islot(c, b, v)
        itake(k, h)
        for dev in devs + [sib]:
            igo(k, h, dev)

    def tpass(o, v, h, devs):
        k = tslot(o, v)
        ttake(k, h)
        for dev in devs:
            tgo(k, h, dev)

    ipass(yb, x_down, 1, [at_x(x_up), by_i])
    tpass(yo, z_down, 1, [at_z(z_up), by_t])
    ipass(1 - yb, x, 0, [at_x(x_up), at_x(x_down)])
    tpass(1 - yo, z, 0, [at_z(z_up), at_z(z_down)])
    ipass(yb, x_up, 1, [by_i])
    tpass(yo, z_up, 1, [by_t])
    ipass(yb, x_up, 0, [at_x(x_down)])
    tpass(yo, z_up, 0, [at_z(z_down)])
    ipass(yb, x_down, 0, [])
    tpass(yo, z_down, 0, [])
    ipass(yb, turn(x, 2), 1, [by_i])
    tpass(yo, turn(z, 2), 1, [by_t])
    ipass(1 - yb, turn(x, 3 - 2 * c), 0, [at_x(turn(x, 1 + 2 * c))])
    tpass(1 - yo, turn(z, 3 - 2 * c), 0, [at_z(turn(z, 1 + 2 * c))])
    ipass(yb, turn(x, 2), 0, [])
    tpass(yo, turn(z, 2), 0, [])

    def tile_logits(q, o):
        rows = pl.ds(pl.multiple_of(q * N * R, N * R), N * R)
        cols = pl.ds(pl.multiple_of(o * N * R, N * R), N * R)
        l = scale2 * lax.dot_general(
            img[rows, :], txt[cols, :], (((1,), (1,)), ((), ())), preferred_element_type=jnp.float32
        )
        logit[rows, cols] = l
        return q, o, cols, l

    def tile_lse(q, o, cols, l):
        rmax = jnp.max(l, axis=1, keepdims=True)
        cmax = jnp.max(l, axis=0, keepdims=True)
        rsum = jnp.sum(jnp.exp2(l - rmax), axis=1, keepdims=True)
        csum = jnp.sum(jnp.exp2(l - cmax), axis=0, keepdims=True)
        rlse = rmax + jnp.log(rsum) * LOG2E
        line = jnp.broadcast_to(rlse, (N * R, R)).T[:1, :]
        for i in range(2):
            rowl[o, pl.ds(2 * q + i, 1), :] = line[:, i * 2 * R : (i + 1) * 2 * R]
        coll[q, :, cols] = cmax + jnp.log(csum) * LOG2E

    def sib_blocks(b):
        for v in range(N):
            for h in range(2):
                itake(islot(1 - c, b, v), h)

    def spot_of(i):
        return lax.rem(c + i, 2) * 2 + lax.rem(yb + i // 4, 2), lax.rem(yo + i // 2, 2)

    def tile_step(i, carry):
        @pl.when(i == 2)
        def _():
            sib_blocks(1 - yb)

        made = [tile_logits(*spot_of(2 * i + u)) for u in range(2)]
        for one in made:
            tile_lse(*one)
        return carry

    tile_lse(*tile_logits(*spot_of(0)))
    sib_blocks(yb)
    tile_lse(*tile_logits(*spot_of(1)))
    ipass(1 - yb, x, 1, [])
    for v in (x_down, x_up):
        ipass(1 - yb, v, 1, [])
    ipass(1 - yb, turn(x, 1 + 2 * c), 0, [])
    ipass(1 - yb, turn(x, 2), 1, [])
    ipass(1 - yb, turn(x, 2), 0, [])
    for v in (z, z_down, z_up, turn(z, 2)):
        tpass(1 - yo, v, 1, [])
    tpass(1 - yo, turn(z, 1 + 2 * c), 0, [])
    tpass(1 - yo, turn(z, 2), 0, [])
    lax.fori_loop(1, N, tile_step, 0)

    rowp[c] = lse2([rowl[0], rowl[1]])
    go(rowp.at[c], rowp.at[c], rp_r.at[c], sib)
    ime, tme = yb * N + x, yo * N + z
    colz[tme] = lse2([coll[q] for q in range(N)])
    for dev in same_t:
        go(colz.at[tme], colz.at[tme], cz_r.at[tme], dev)
    take(rowp.at[1 - c], rp_r.at[1 - c])
    rowx[ime] = lse2([rowp[0], rowp[1]])
    for dev in same_i:
        go(rowx.at[ime], rowx.at[ime], rx_r.at[ime], dev)

    def others(b, v):
        return [b * N + turn(v, d) for d in range(1, N)] + [(1 - b) * N + turn(v, d) for d in range(N)]

    for t in others(yo, z):
        take(colz.at[t], cz_r.at[t])
    coll[0] = lse2([colz[v] for v in range(2 * N)])
    for t in others(yb, x):
        take(rowx.at[t], rx_r.at[t])
    rowl[0] = lse2([rowx[v] for v in range(2 * N)])

    lane = lax.broadcasted_iota(jnp.int32, (8, R), 1)

    def meets(k):
        irow = k % N * 2 + k // (2 * N)
        icol = (yo * 2 + k // N % 2) * N + z
        trow, tcol = icol % (2 * N), irow * 2 + icol // (2 * N)
        ty = tcol // N
        here = jnp.logical_and(trow == row, jnp.logical_or(ty == y, ty == yt))
        return here, tslot(ty // 2, tcol % N)

    def delta_part(p, total):
        l = logit[pair(p), :]
        rcol = jnp.broadcast_to(rowl[0, pl.ds(p, 1), :], (R, 2 * R)).T[:, :1]
        target = lax.broadcasted_iota(jnp.int32, (2 * R, 1), 0)
        offs = []
        for i in range(2):
            here, slot = meets(2 * p + i)
            offs.append(jnp.where(here, (slot - i) * R, -4 * TEXTS))
        target = target + jnp.where(target < R, offs[0], offs[1])
        twice = jnp.where(lax.broadcasted_iota(jnp.int32, (2 * R, TEXTS), 1) == target, 2.0, 0.0)
        d = jnp.exp2(l - rcol) + jnp.exp2(l - coll[0]) - twice
        total = total + jnp.sum(d * l, axis=0, keepdims=True)
        low = d.astype(jnp.bfloat16)
        delta[pair(p), :] = low
        return low, total

    def image_part(low):
        return jnp.dot(low, txt[...], preferred_element_type=jnp.float32)

    def sum_go(level, at, devs):
        for dev in devs:
            go(sums.at[level, at], sums.at[level, at], su_r.at[level, at], dev)

    def sum_take(level, at):
        take(sums.at[level, at], su_r.at[level, at])

    ring_me, pair_me = (x, z), (yb, yo)
    ring_at, partner = (at_x, at_z), (by_i, by_t)
    stages = (stage_i, stage_t)

    def h0_copy(m, g, b, v):
        return send(
            stages[m].at[half(g, 0), :], a0.at[m, ring_me[m], b], pa0_s.at[m, g],
            pa0_r.at[m, ring_me[m], b], ring_at[m](v),
        )

    def h1_copy(m, g, v):
        return send(stages[m].at[half(g, 1), :], a1.at[m, v], pa1_s.at[m, g], pa1_r.at[m, v], partner[m])

    def spot(m, i):
        b = pair_me[m] if i // 2 else 1 - pair_me[m]
        near = ring_me[m] // 2
        return b, near if i % 2 else 1 - near

    def order(m, i):
        b, half_ring = spot(m, i)
        return b * 2 + half_ring

    def twin(m):
        return ring_me[m] + 1 - ring_me[m] % 2 * 2

    def emit(m, i, part):
        b, half_ring = spot(m, i)
        stages[m][pair(order(m, i)), :] = part.astype(jnp.bfloat16)
        for t in range(2):
            v = 2 * half_ring + t
            if i % 2:
                own0[m, i // 2, t] = part[t * R : t * R + H, :]
            else:
                h0_copy(m, b * N + v, b, v).start()
            if i // 2:
                own1[m, v] = part[t * R + H : (t + 1) * R, :]
            else:
                h1_copy(m, b * N + v, v).start()
        if i % 2:
            h0_copy(m, b * N + twin(m), b, twin(m)).start()

    def sib_copy(j):
        return send(stage_s.at[pair(j), :], stage_c.at[pair(j), :], qc_s.at[j], qc_r.at[j], sib)

    def sib_part(i, total):
        j = order(0, i)
        low, total = delta_part((1 - c) * N + j, total)
        stage_s[pair(j), :] = image_part(low).astype(jnp.bfloat16)
        return total

    total = jnp.zeros((1, TEXTS), jnp.float32)
    for i in range(2):
        total = sib_part(i, total)
    for i in range(2):
        sib_copy(order(0, i)).start()
    for i in range(2, N):
        total = sib_part(i, total)

    def image_emit(i, parts):
        for u in range(2):
            j = order(0, i + u)
            sib_copy(j).wait_recv()
            emit(0, i + u, parts[u] + stage_c[pair(j), :].astype(jnp.float32))

    def text_emit(i, count):
        parts = [
            lax.dot_general(
                delta[:, pair(order(1, i + u))], img[...], (((0,), (0,)), ((), ())),
                preferred_element_type=jnp.float32,
            )
            for u in range(count)
        ]
        for u in range(count):
            emit(1, i + u, parts[u])

    parts = []
    for i in range(2):
        low, total = delta_part(c * N + order(0, i), total)
        parts.append(image_part(low))
    for i in range(2, N):
        total = delta_part(c * N + order(0, i), total)[1]
    for i in range(2, N):
        sib_copy(order(0, i)).start()
    image_emit(0, parts)
    sums[0, c] = jnp.where(lane == 1, jnp.sum(total, axis=1, keepdims=True), jnp.zeros((8, R), jnp.float32))
    eye = lax.broadcasted_iota(jnp.int32, (R, R), 0) == lax.broadcasted_iota(jnp.int32, (R, R), 1)

    def loss_step(k, carry):
        here, slot = meets(k)

        @pl.when(here)
        def _():
            cols = block(slot)
            both = rowl[0, pl.ds(k // 2, 1), :]
            rl = jnp.where(k % 2 == 0, both[:, :R], both[:, R:])
            pairs = jnp.sum(jnp.where(eye, logit[block(k), cols], 0.0), axis=0, keepdims=True)
            part = jnp.sum(rl + coll[0, :, cols] - 2.0 * pairs, axis=1, keepdims=True)
            sums[0, c] = sums[0, c] + jnp.where(lane == 0, part, 0.0)

        return carry

    lax.fori_loop(0, N * N, loss_step, 0)
    sum_go(0, c, [sib])

    text_emit(0, 1)
    text_emit(1, 1)
    sum_take(0, 1 - c)
    sums[1, ime] = sums[0, 0] + sums[0, 1]
    sum_go(1, ime, same_i)
    image_emit(2, [image_part(delta[pair(c * N + order(0, i)), :]) for i in range(2, N)])
    text_emit(2, 2)


    def h0_sum(m, i):
        b = pair_me[m] if i else 1 - pair_me[m]
        acc = own0[m, i, ring_me[m] % 2]
        for d in range(1, N):
            s = turn(ring_me[m], d)
            take(a0.at[m, s, b], pa0_r.at[m, s, b])
            acc = acc + a0[m, s, b].astype(jnp.float32)
        return acc

    def h1_sum(m, v):
        take(a1.at[m, v], pa1_r.at[m, v])
        return own1[m, v] + a1[m, v].astype(jnp.float32)

    def second0(m):
        sb[m, N] = h0_sum(m, 0).astype(jnp.bfloat16)
        go(sb.at[m, N], b0.at[m], pb0_r.at[m], partner[m])

    def second1(m, v):
        sb[m, v] = h1_sum(m, v).astype(jnp.bfloat16)
        go(sb.at[m, v], b1.at[m, ring_me[m]], pb1_r.at[m, ring_me[m]], ring_at[m](v))

    def far_blocks(m):
        v = 2 - ring_me[m] // 2 * 2
        return v, v + 1

    for v in far_blocks(0):
        second1(0, v)
    for t in others(yb, x):
        sum_take(1, t)
    acc = sums[1, 0]
    for v in range(1, 2 * N):
        acc = acc + sums[1, v]
    sums[2, tme] = acc
    sum_go(2, tme, same_t)
    second0(0)
    for v in far_blocks(1):
        second1(1, v)
    second1(0, twin(0))
    second0(1)
    second1(1, twin(1))
    for m in range(2):
        fin[m, 0] = h0_sum(m, 1)
        fin[m, 1] = h1_sum(m, ring_me[m])

    factor = scale * (1.0 / (2.0 * TEXTS * N * N))
    sources, results = (img_ref, txt_ref), (gi_ref, gt_ref)
    for m in range(2):
        take(b0.at[m], pb0_r.at[m])
        acc = fin[m, 0] + b0[m].astype(jnp.float32)
        results[m][:H, :] = project(sources[m][:H, :], factor * acc)
        acc = fin[m, 1]
        for d in range(1, N):
            s = turn(ring_me[m], d)
            take(b1.at[m, s], pb1_r.at[m, s])
            acc = acc + b1[m, s].astype(jnp.float32)
        results[m][H:, :] = project(sources[m][H:, :], factor * acc)
    for t in others(yo, z):
        sum_take(2, t)
    whole = sums[2, 0]
    for v in range(1, 2 * N):
        whole = whole + sums[2, v]
    whole = whole * (LN2 / (2.0 * TEXTS * N * N))
    top = lax.broadcasted_iota(jnp.int32, (8, R), 0) == 0
    loss_ref[0] = jnp.sum(jnp.where(jnp.logical_and(top, lane == 0), whole, 0.0))
    gs_ref[0] = jnp.sum(jnp.where(jnp.logical_and(top, lane == 1), whole, 0.0))

    for copy in started:
        copy.wait_send()

    for m in range(2):
        for b in range(2):
            for d in range(1, N):
                v = turn(ring_me[m], d)
                h0_copy(m, b * N + v, b, v).wait_send()
        for v in range(N):
            h1_copy(m, (1 - pair_me[m]) * N + v, v).wait_send()
    for j in range(N):
        sib_copy(j).wait_send()


def local(images, texts, log_scale):
    f32, bf16 = jnp.float32, jnp.bfloat16
    dma = pltpu.SemaphoreType.DMA
    vmem = pl.BlockSpec(memory_space=pltpu.VMEM)
    smem = pl.BlockSpec(memory_space=pltpu.SMEM)
    gi, gt, loss, gs = pl.pallas_call(
        kernel,
        out_shape=(
            jax.ShapeDtypeStruct((R, E), f32),
            jax.ShapeDtypeStruct((R, E), f32),
            jax.ShapeDtypeStruct((1,), f32),
            jax.ShapeDtypeStruct((1,), f32),
        ),
        in_specs=[vmem, vmem, smem],
        out_specs=(vmem, vmem, smem, smem),
        scratch_shapes=[
            pltpu.VMEM((IMAGES, E), bf16),
            pltpu.VMEM((TEXTS, E), bf16),
            pltpu.VMEM((IMAGES, TEXTS), f32),
            pltpu.VMEM((IMAGES, TEXTS), bf16),
            pltpu.VMEM((TEXTS, E), bf16),
            pltpu.VMEM((TEXTS, E), bf16),
            pltpu.VMEM((TEXTS, E), bf16),
            pltpu.VMEM((TEXTS, E), bf16),
            pltpu.VMEM((2, 2, 2, H, E), f32),
            pltpu.VMEM((2, N, H, E), f32),
            pltpu.VMEM((2, 2, H, E), f32),
            pltpu.VMEM((2, N, 2, H, E), bf16),
            pltpu.VMEM((2, N, H, E), bf16),
            pltpu.VMEM((2, N + 1, H, E), bf16),
            pltpu.VMEM((2, H, E), bf16),
            pltpu.VMEM((2, N, H, E), bf16),
            pltpu.VMEM((2, PAIRS, 2 * R), f32),
            pltpu.VMEM((2, PAIRS, 2 * R), f32),
            pltpu.VMEM((2 * N, PAIRS, 2 * R), f32),
            pltpu.VMEM((N, 1, TEXTS), f32),
            pltpu.VMEM((2 * N, 1, TEXTS), f32),
            pltpu.VMEM((3, 2 * N, 8, R), f32),
            dma((96,)),
            dma((N * N, 2)),
            dma((2 * N, 2)),
            dma((2,)), dma((2 * N,)), dma((2 * N,)),
            dma((N,)), dma((N,)),
            dma((2, 2 * N)), dma((2, 2 * N)),
            dma((2, N, 2)), dma((2, N)),
            dma((2,)), dma((2, N)),
            dma((3, 2 * N)),
        ],
        compiler_params=pltpu.CompilerParams(
            collective_id=0, has_side_effects=True, vmem_limit_bytes=56 * 1024 * 1024
        ),
    )(images, texts, log_scale.reshape(1))
    return gi, gt, loss.reshape(()), gs.reshape(())


def solution(mesh):
    placed = (P(("row", "col"), None), P(("col", "row"), None), P())
    return jax.shard_map(
        local,
        mesh=mesh,
        in_specs=placed,
        out_specs=(P(("row", "col"), None), P(("col", "row"), None), P(), P()),
        check_vma=False,
    )
```

```python
import math

import jax
import jax.numpy as jnp
from jax import lax
from jax.experimental import pallas as pl
from jax.experimental.pallas import tpu as pltpu
from jax.sharding import PartitionSpec as P

EPS = 1e-06
LOG2E = math.log2(math.e)
LN2 = math.log(2.0)
MESH = pl.DeviceIdType.MESH
N = 4
R = 128
H = R // 2
E = 768
IMAGES = N * N * R
TEXTS = 2 * N * R
PAIRS = IMAGES // (2 * R)


def unit_rows(values):
    full = values.astype(jnp.float32)
    inverse = lax.rsqrt(jnp.sum(full * full, axis=1, keepdims=True) + EPS)
    return full * inverse, inverse


def lse2(values):
    peak = values[0]
    for v in values[1:]:
        peak = jnp.maximum(peak, v)
    total = jnp.exp2(values[0] - peak)
    for v in values[1:]:
        total = total + jnp.exp2(v - peak)
    return peak + jnp.log(total) * LOG2E


def project(values, grad):
    unit, inverse = unit_rows(values)
    return inverse * (grad - unit * jnp.sum(unit * grad, axis=1, keepdims=True))


def kernel(
    img_ref, txt_ref, scale_ref, sum_ref, whole_ref,
    img, txt, logit, delta, stage_s, stage_c, stage_i, stage_t,
    own0, own1, fin, a0, a1, sb, b0, b1,
    rowl, rowp, rowx, coll, colz, sums,
    g_s, g_r, t_r, rp_r, rx_r, cz_r, qc_s, qc_r, pa0_s, pa1_s, pa0_r, pa1_r, pb0_r, pb1_r, su_r,
):
    row, col = lax.axis_index("row"), lax.axis_index("col")
    x, c = row // 2, row % 2
    y, z = col // N, col % N
    yb, yo = y % 2, y // 2
    yi = y + 1 - 2 * yb
    yt = N - 1 - y
    sib = (row + 1 - 2 * c, col)
    by_i = (row, yi * N + z)
    by_t = (row, yt * N + z)
    def at_x(v):
        return (v * 2 + c, col)

    def at_z(v):
        return (row, y * N + v)

    def turn(v, d):
        return lax.rem(v + d, N)

    x_up, x_down, z_up, z_down = turn(x, 1), turn(x, 3), turn(z, 1), turn(z, 3)

    same_i = [at_x(turn(x, d)) for d in range(1, N)]
    same_i += [(turn(x, d) * 2 + c, yi * N + z) for d in (1, 3, 2)] + [by_i]
    same_t = [at_z(turn(z, d)) for d in range(1, N)]
    same_t += [(row, yt * N + turn(z, d)) for d in (1, 3, 2)] + [by_t]

    def send(src, dst, ssem, rsem, dev):
        return pltpu.make_async_remote_copy(
            src_ref=src, dst_ref=dst, send_sem=ssem, recv_sem=rsem, device_id=dev, device_id_type=MESH
        )

    started = []

    def go(src, dst, rsem, dev):
        copy = send(src, dst, g_s.at[len(started)], rsem, dev)
        copy.start()
        started.append(copy)

    def take(dst, rsem):
        send(dst, dst, g_s.at[0], rsem, sib).wait_recv()

    barrier = pltpu.get_barrier_semaphore()
    peers = [at_x(x_up), at_x(x_down), at_z(z_up), at_z(z_down), by_i, by_t, sib]
    for dev in peers:
        pl.semaphore_signal(barrier, inc=1, device_id=dev, device_id_type=MESH)

    def block(k):
        return pl.ds(pl.multiple_of(k * R, R), R)

    def pair(p):
        return pl.ds(pl.multiple_of(p * 2 * R, 2 * R), 2 * R)

    def half(k, h):
        return pl.ds(pl.multiple_of(k * R + h * H, H), H)

    def islot(cc, b, xx):
        return cc * 2 * N + b * N + xx

    def tslot(o, zz):
        return o * N + zz

    imine, tmine = islot(c, yb, x), tslot(yo, z)
    img[block(imine), :] = unit_rows(img_ref[...])[0].astype(jnp.bfloat16)
    txt[block(tmine), :] = unit_rows(txt_ref[...])[0].astype(jnp.bfloat16)
    scale = jnp.exp(jnp.full((1, 1), scale_ref[0], jnp.float32))
    scale2 = scale * LOG2E
    pl.semaphore_wait(barrier, len(peers))

    def iview(k, h):
        return img.at[half(k, h), :]

    def tview(k, h):
        return txt.at[half(k, h), :]

    def igo(k, h, dev):
        go(iview(k, h), iview(k, h), g_r.at[k, h], dev)

    def tgo(k, h, dev):
        go(tview(k, h), tview(k, h), t_r.at[k, h], dev)

    def itake(k, h):
        take(iview(k, h), g_r.at[k, h])

    def ttake(k, h):
        take(tview(k, h), t_r.at[k, h])

    igo(imine, 0, by_i)
    tgo(tmine, 0, by_t)
    for h in (1, 0):
        for v, w in ((x_up, z_up), (x_down, z_down)):
            igo(imine, h, at_x(v))
            tgo(tmine, h, at_z(w))
    igo(imine, 1, by_i)
    tgo(tmine, 1, by_t)
    for h in range(2):
        igo(imine, h, sib)

    def ipass(b, v, h, devs):
        k = islot(c, b, v)
        itake(k, h)
        for dev in devs + [sib]:
            igo(k, h, dev)

    def tpass(o, v, h, devs):
        k = tslot(o, v)
        ttake(k, h)
        for dev in devs:
            tgo(k, h, dev)

    ipass(yb, x_down, 1, [at_x(x_up), by_i])
    tpass(yo, z_down, 1, [at_z(z_up), by_t])
    ipass(1 - yb, x, 0, [at_x(x_up), at_x(x_down)])
    tpass(1 - yo, z, 0, [at_z(z_up), at_z(z_down)])
    ipass(yb, x_up, 1, [by_i])
    tpass(yo, z_up, 1, [by_t])
    ipass(yb, x_up, 0, [at_x(x_down)])
    tpass(yo, z_up, 0, [at_z(z_down)])
    ipass(yb, x_down, 0, [])
    tpass(yo, z_down, 0, [])
    ipass(yb, turn(x, 2), 1, [by_i])
    tpass(yo, turn(z, 2), 1, [by_t])
    ipass(1 - yb, turn(x, 3 - 2 * c), 0, [at_x(turn(x, 1 + 2 * c))])
    tpass(1 - yo, turn(z, 3 - 2 * c), 0, [at_z(turn(z, 1 + 2 * c))])
    ipass(yb, turn(x, 2), 0, [])
    tpass(yo, turn(z, 2), 0, [])

    def tile_logits(q, o):
        rows = pl.ds(pl.multiple_of(q * N * R, N * R), N * R)
        cols = pl.ds(pl.multiple_of(o * N * R, N * R), N * R)
        l = scale2 * lax.dot_general(
            img[rows, :], txt[cols, :], (((1,), (1,)), ((), ())), preferred_element_type=jnp.float32
        )
        logit[rows, cols] = l
        return q, o, cols, l

    def tile_lse(q, o, cols, l):
        rmax = jnp.max(l, axis=1, keepdims=True)
        cmax = jnp.max(l, axis=0, keepdims=True)
        rsum = jnp.sum(jnp.exp2(l - rmax), axis=1, keepdims=True)
        csum = jnp.sum(jnp.exp2(l - cmax), axis=0, keepdims=True)
        rlse = rmax + jnp.log(rsum) * LOG2E
        line = jnp.broadcast_to(rlse, (N * R, R)).T[:1, :]
        for i in range(2):
            rowl[o, pl.ds(2 * q + i, 1), :] = line[:, i * 2 * R : (i + 1) * 2 * R]
        coll[q, :, cols] = cmax + jnp.log(csum) * LOG2E

    def sib_blocks(b):
        for v in range(N):
            for h in range(2):
                itake(islot(1 - c, b, v), h)

    def spot_of(i):
        return lax.rem(c + i, 2) * 2 + lax.rem(yb + i // 4, 2), lax.rem(yo + i // 2, 2)

    def tile_step(i, carry):
        @pl.when(i == 2)
        def _():
            sib_blocks(1 - yb)

        made = [tile_logits(*spot_of(2 * i + u)) for u in range(2)]
        for one in made:
            tile_lse(*one)
        return carry

    tile_lse(*tile_logits(*spot_of(0)))
    sib_blocks(yb)
    tile_lse(*tile_logits(*spot_of(1)))
    ipass(1 - yb, x, 1, [])
    for v in (x_down, x_up):
        ipass(1 - yb, v, 1, [])
    ipass(1 - yb, turn(x, 1 + 2 * c), 0, [])
    ipass(1 - yb, turn(x, 2), 1, [])
    ipass(1 - yb, turn(x, 2), 0, [])
    for v in (z, z_down, z_up, turn(z, 2)):
        tpass(1 - yo, v, 1, [])
    tpass(1 - yo, turn(z, 1 + 2 * c), 0, [])
    tpass(1 - yo, turn(z, 2), 0, [])
    lax.fori_loop(1, N, tile_step, 0)

    rowp[c] = lse2([rowl[0], rowl[1]])
    go(rowp.at[c], rowp.at[c], rp_r.at[c], sib)
    ime, tme = yb * N + x, yo * N + z
    colz[tme] = lse2([coll[q] for q in range(N)])
    for dev in same_t:
        go(colz.at[tme], colz.at[tme], cz_r.at[tme], dev)
    take(rowp.at[1 - c], rp_r.at[1 - c])
    rowx[ime] = lse2([rowp[0], rowp[1]])
    for dev in same_i:
        go(rowx.at[ime], rowx.at[ime], rx_r.at[ime], dev)

    def others(b, v):
        return [b * N + turn(v, d) for d in range(1, N)] + [(1 - b) * N + turn(v, d) for d in range(N)]

    for t in others(yo, z):
        take(colz.at[t], cz_r.at[t])
    coll[0] = lse2([colz[v] for v in range(2 * N)])
    for t in others(yb, x):
        take(rowx.at[t], rx_r.at[t])
    rowl[0] = lse2([rowx[v] for v in range(2 * N)])

    lane = lax.broadcasted_iota(jnp.int32, (8, R), 1)

    def meets(k):
        irow = k % N * 2 + k // (2 * N)
        icol = (yo * 2 + k // N % 2) * N + z
        trow, tcol = icol % (2 * N), irow * 2 + icol // (2 * N)
        ty = tcol // N
        here = jnp.logical_and(trow == row, jnp.logical_or(ty == y, ty == yt))
        return here, tslot(ty // 2, tcol % N)

    def delta_part(p, total):
        l = logit[pair(p), :]
        rcol = jnp.broadcast_to(rowl[0, pl.ds(p, 1), :], (R, 2 * R)).T[:, :1]
        target = lax.broadcasted_iota(jnp.int32, (2 * R, 1), 0)
        offs = []
        for i in range(2):
            here, slot = meets(2 * p + i)
            offs.append(jnp.where(here, (slot - i) * R, -4 * TEXTS))
        target = target + jnp.where(target < R, offs[0], offs[1])
        twice = jnp.where(lax.broadcasted_iota(jnp.int32, (2 * R, TEXTS), 1) == target, 2.0, 0.0)
        d = jnp.exp2(l - rcol) + jnp.exp2(l - coll[0]) - twice
        total = total + jnp.sum(d * l, axis=0, keepdims=True)
        low = d.astype(jnp.bfloat16)
        delta[pair(p), :] = low
        return low, total

    def image_part(low):
        return jnp.dot(low, txt[...], preferred_element_type=jnp.float32)

    def sum_go(level, at, devs):
        for dev in devs:
            go(sums.at[level, at], sums.at[level, at], su_r.at[level, at], dev)

    def sum_take(level, at):
        take(sums.at[level, at], su_r.at[level, at])

    ring_me, pair_me = (x, z), (yb, yo)
    ring_at, partner = (at_x, at_z), (by_i, by_t)
    stages = (stage_i, stage_t)

    def h0_copy(m, g, b, v):
        return send(
            stages[m].at[half(g, 0), :], a0.at[m, ring_me[m], b], pa0_s.at[m, g],
            pa0_r.at[m, ring_me[m], b], ring_at[m](v),
        )

    def h1_copy(m, g, v):
        return send(stages[m].at[half(g, 1), :], a1.at[m, v], pa1_s.at[m, g], pa1_r.at[m, v], partner[m])

    def spot(m, i):
        b = pair_me[m] if i // 2 else 1 - pair_me[m]
        near = ring_me[m] // 2
        return b, near if i % 2 else 1 - near

    def order(m, i):
        b, half_ring = spot(m, i)
        return b * 2 + half_ring

    def twin(m):
        return ring_me[m] + 1 - ring_me[m] % 2 * 2

    def emit(m, i, part):
        b, half_ring = spot(m, i)
        stages[m][pair(order(m, i)), :] = part.astype(jnp.bfloat16)
        for t in range(2):
            v = 2 * half_ring + t
            if i % 2:
                own0[m, i // 2, t] = part[t * R : t * R + H, :]
            else:
                h0_copy(m, b * N + v, b, v).start()
            if i // 2:
                own1[m, v] = part[t * R + H : (t + 1) * R, :]
            else:
                h1_copy(m, b * N + v, v).start()
        if i % 2:
            h0_copy(m, b * N + twin(m), b, twin(m)).start()

    def sib_copy(j):
        return send(stage_s.at[pair(j), :], stage_c.at[pair(j), :], qc_s.at[j], qc_r.at[j], sib)

    def sib_part(i, total):
        j = order(0, i)
        low, total = delta_part((1 - c) * N + j, total)
        stage_s[pair(j), :] = image_part(low).astype(jnp.bfloat16)
        return total

    total = jnp.zeros((1, TEXTS), jnp.float32)
    for i in range(2):
        total = sib_part(i, total)
    for i in range(2):
        sib_copy(order(0, i)).start()
    for i in range(2, N):
        total = sib_part(i, total)

    def image_emit(i, parts):
        for u in range(2):
            j = order(0, i + u)
            sib_copy(j).wait_recv()
            emit(0, i + u, parts[u] + stage_c[pair(j), :].astype(jnp.float32))

    def text_emit(i, count):
        parts = [
            lax.dot_general(
                delta[:, pair(order(1, i + u))], img[...], (((0,), (0,)), ((), ())),
                preferred_element_type=jnp.float32,
            )
            for u in range(count)
        ]
        for u in range(count):
            emit(1, i + u, parts[u])

    parts = []
    for i in range(2):
        low, total = delta_part(c * N + order(0, i), total)
        parts.append(image_part(low))
    for i in range(2, N):
        total = delta_part(c * N + order(0, i), total)[1]
    for i in range(2, N):
        sib_copy(order(0, i)).start()
    image_emit(0, parts)
    sums[0, c] = jnp.where(lane == 1, jnp.sum(total, axis=1, keepdims=True), jnp.zeros((8, R), jnp.float32))
    eye = lax.broadcasted_iota(jnp.int32, (R, R), 0) == lax.broadcasted_iota(jnp.int32, (R, R), 1)

    def loss_step(k, carry):
        here, slot = meets(k)

        @pl.when(here)
        def _():
            cols = block(slot)
            both = rowl[0, pl.ds(k // 2, 1), :]
            rl = jnp.where(k % 2 == 0, both[:, :R], both[:, R:])
            pairs = jnp.sum(jnp.where(eye, logit[block(k), cols], 0.0), axis=0, keepdims=True)
            part = jnp.sum(rl + coll[0, :, cols] - 2.0 * pairs, axis=1, keepdims=True)
            sums[0, c] = sums[0, c] + jnp.where(lane == 0, part, 0.0)

        return carry

    lax.fori_loop(0, N * N, loss_step, 0)
    sum_go(0, c, [sib])

    text_emit(0, 1)
    text_emit(1, 1)
    sum_take(0, 1 - c)
    sums[1, ime] = sums[0, 0] + sums[0, 1]
    sum_go(1, ime, same_i)
    image_emit(2, [image_part(delta[pair(c * N + order(0, i)), :]) for i in range(2, N)])
    text_emit(2, 2)


    def h0_sum(m, i):
        b = pair_me[m] if i else 1 - pair_me[m]
        acc = own0[m, i, ring_me[m] % 2]
        for d in range(1, N):
            s = turn(ring_me[m], d)
            take(a0.at[m, s, b], pa0_r.at[m, s, b])
            acc = acc + a0[m, s, b].astype(jnp.float32)
        return acc

    def h1_sum(m, v):
        take(a1.at[m, v], pa1_r.at[m, v])
        return own1[m, v] + a1[m, v].astype(jnp.float32)

    def second0(m):
        sb[m, N] = h0_sum(m, 0).astype(jnp.bfloat16)
        go(sb.at[m, N], b0.at[m], pb0_r.at[m], partner[m])

    def second1(m, v):
        sb[m, v] = h1_sum(m, v).astype(jnp.bfloat16)
        go(sb.at[m, v], b1.at[m, ring_me[m]], pb1_r.at[m, ring_me[m]], ring_at[m](v))

    def far_blocks(m):
        v = 2 - ring_me[m] // 2 * 2
        return v, v + 1

    for v in far_blocks(0):
        second1(0, v)
    for t in others(yb, x):
        sum_take(1, t)
    acc = sums[1, 0]
    for v in range(1, 2 * N):
        acc = acc + sums[1, v]
    sums[2, tme] = acc
    sum_go(2, tme, same_t)
    second0(0)
    for v in far_blocks(1):
        second1(1, v)
    second1(0, twin(0))
    second0(1)
    second1(1, twin(1))
    for m in range(2):
        fin[m, 0] = h0_sum(m, 1)
        fin[m, 1] = h1_sum(m, ring_me[m])

    factor = scale * (1.0 / (2.0 * TEXTS * N * N))
    for m in range(2):
        take(b0.at[m], pb0_r.at[m])
        acc = fin[m, 0] + b0[m].astype(jnp.float32)
        sum_ref[m, :H, :] = factor * acc
        acc = fin[m, 1]
        for d in range(1, N):
            s = turn(ring_me[m], d)
            take(b1.at[m, s], pb1_r.at[m, s])
            acc = acc + b1[m, s].astype(jnp.float32)
        sum_ref[m, H:, :] = factor * acc
    for t in others(yo, z):
        sum_take(2, t)
    whole = sums[2, 0]
    for v in range(1, 2 * N):
        whole = whole + sums[2, v]
    whole = whole * (LN2 / (2.0 * TEXTS * N * N))
    whole_ref[...] = whole

    for copy in started:
        copy.wait_send()

    for m in range(2):
        for b in range(2):
            for d in range(1, N):
                v = turn(ring_me[m], d)
                h0_copy(m, b * N + v, b, v).wait_send()
        for v in range(N):
            h1_copy(m, (1 - pair_me[m]) * N + v, v).wait_send()
    for j in range(N):
        sib_copy(j).wait_send()


def finish(img_ref, txt_ref, sum_ref, whole_ref, gi_ref, gt_ref, loss_ref, gs_ref):
    gi_ref[...] = project(img_ref[...], sum_ref[0])
    gt_ref[...] = project(txt_ref[...], sum_ref[1])
    whole = whole_ref[...]
    lane = lax.broadcasted_iota(jnp.int32, (8, R), 1)
    top = lax.broadcasted_iota(jnp.int32, (8, R), 0) == 0
    loss_ref[0] = jnp.sum(jnp.where(jnp.logical_and(top, lane == 0), whole, 0.0))
    gs_ref[0] = jnp.sum(jnp.where(jnp.logical_and(top, lane == 1), whole, 0.0))


def local(images, texts, log_scale):
    f32, bf16 = jnp.float32, jnp.bfloat16
    dma = pltpu.SemaphoreType.DMA
    vmem = pl.BlockSpec(memory_space=pltpu.VMEM)
    smem = pl.BlockSpec(memory_space=pltpu.SMEM)
    sums, whole = pl.pallas_call(
        kernel,
        out_shape=(jax.ShapeDtypeStruct((2, R, E), f32), jax.ShapeDtypeStruct((8, R), f32)),
        in_specs=[vmem, vmem, smem],
        out_specs=(vmem, vmem),
        scratch_shapes=[
            pltpu.VMEM((IMAGES, E), bf16),
            pltpu.VMEM((TEXTS, E), bf16),
            pltpu.VMEM((IMAGES, TEXTS), f32),
            pltpu.VMEM((IMAGES, TEXTS), bf16),
            pltpu.VMEM((TEXTS, E), bf16),
            pltpu.VMEM((TEXTS, E), bf16),
            pltpu.VMEM((TEXTS, E), bf16),
            pltpu.VMEM((TEXTS, E), bf16),
            pltpu.VMEM((2, 2, 2, H, E), f32),
            pltpu.VMEM((2, N, H, E), f32),
            pltpu.VMEM((2, 2, H, E), f32),
            pltpu.VMEM((2, N, 2, H, E), bf16),
            pltpu.VMEM((2, N, H, E), bf16),
            pltpu.VMEM((2, N + 1, H, E), bf16),
            pltpu.VMEM((2, H, E), bf16),
            pltpu.VMEM((2, N, H, E), bf16),
            pltpu.VMEM((2, PAIRS, 2 * R), f32),
            pltpu.VMEM((2, PAIRS, 2 * R), f32),
            pltpu.VMEM((2 * N, PAIRS, 2 * R), f32),
            pltpu.VMEM((N, 1, TEXTS), f32),
            pltpu.VMEM((2 * N, 1, TEXTS), f32),
            pltpu.VMEM((3, 2 * N, 8, R), f32),
            dma((96,)),
            dma((N * N, 2)),
            dma((2 * N, 2)),
            dma((2,)), dma((2 * N,)), dma((2 * N,)),
            dma((N,)), dma((N,)),
            dma((2, 2 * N)), dma((2, 2 * N)),
            dma((2, N, 2)), dma((2, N)),
            dma((2,)), dma((2, N)),
            dma((3, 2 * N)),
        ],
        compiler_params=pltpu.CompilerParams(
            collective_id=0, has_side_effects=True, vmem_limit_bytes=56 * 1024 * 1024
        ),
    )(images, texts, log_scale.reshape(1))
    gi, gt, loss, gs = pl.pallas_call(
        finish,
        out_shape=(
            jax.ShapeDtypeStruct((R, E), f32),
            jax.ShapeDtypeStruct((R, E), f32),
            jax.ShapeDtypeStruct((1,), f32),
            jax.ShapeDtypeStruct((1,), f32),
        ),
        in_specs=[vmem, vmem, vmem, vmem],
        out_specs=(vmem, vmem, smem, smem),
    )(images, texts, sums, whole)
    return gi, gt, loss.reshape(()), gs.reshape(())


def solution(mesh):
    placed = (P(("row", "col"), None), P(("col", "row"), None), P())
    return jax.shard_map(
        local,
        mesh=mesh,
        in_specs=placed,
        out_specs=(P(("row", "col"), None), P(("col", "row"), None), P(), P()),
        check_vma=False,
    )
```

```python
import math

import jax
import jax.numpy as jnp
from jax import lax
from jax.experimental import pallas as pl
from jax.experimental.pallas import tpu as pltpu
from jax.sharding import PartitionSpec as P

EPS = 1e-06
LOG2E = math.log2(math.e)
LN2 = math.log(2.0)
MESH = pl.DeviceIdType.MESH
N = 4
R = 128
H = R // 2
E = 768
IMAGES = N * N * R
TEXTS = 2 * N * R
PAIRS = IMAGES // (2 * R)


def unit_rows(values):
    full = values.astype(jnp.float32)
    inverse = lax.rsqrt(jnp.sum(full * full, axis=1, keepdims=True) + EPS)
    return full * inverse, inverse


def lse2(values):
    peak = values[0]
    for v in values[1:]:
        peak = jnp.maximum(peak, v)
    total = jnp.exp2(values[0] - peak)
    for v in values[1:]:
        total = total + jnp.exp2(v - peak)
    return peak + jnp.log(total) * LOG2E


def project(values, grad):
    unit, inverse = unit_rows(values)
    return inverse * (grad - unit * jnp.sum(unit * grad, axis=1, keepdims=True))


def kernel(
    img_ref, txt_ref, scale_ref, sum_ref, whole_ref,
    img, txt, logit, delta, stage_s, stage_c, stage_i, stage_t,
    own0, own1, fin, a0, a1, sb, b0, b1,
    rowl, rowp, rowx, coll, colz, sums,
    g_s, g_r, t_r, rp_r, rx_r, cz_r, qc_s, qc_r, pa0_s, pa1_s, pa0_r, pa1_r, pb0_r, pb1_r, su_r,
):
    row, col = lax.axis_index("row"), lax.axis_index("col")
    x, c = row // 2, row % 2
    y, z = col // N, col % N
    yb, yo = y % 2, y // 2
    yi = y + 1 - 2 * yb
    yt = N - 1 - y
    sib = (row + 1 - 2 * c, col)
    by_i = (row, yi * N + z)
    by_t = (row, yt * N + z)
    def at_x(v):
        return (v * 2 + c, col)

    def at_z(v):
        return (row, y * N + v)

    def turn(v, d):
        return lax.rem(v + d, N)

    x_up, x_down, z_up, z_down = turn(x, 1), turn(x, 3), turn(z, 1), turn(z, 3)

    same_i = [at_x(turn(x, d)) for d in range(1, N)]
    same_i += [(turn(x, d) * 2 + c, yi * N + z) for d in (1, 3, 2)] + [by_i]
    same_t = [at_z(turn(z, d)) for d in range(1, N)]
    same_t += [(row, yt * N + turn(z, d)) for d in (1, 3, 2)] + [by_t]

    def send(src, dst, ssem, rsem, dev):
        return pltpu.make_async_remote_copy(
            src_ref=src, dst_ref=dst, send_sem=ssem, recv_sem=rsem, device_id=dev, device_id_type=MESH
        )

    started = []

    def go(src, dst, rsem, dev):
        copy = send(src, dst, g_s.at[len(started)], rsem, dev)
        copy.start()
        started.append(copy)

    def take(dst, rsem):
        send(dst, dst, g_s.at[0], rsem, sib).wait_recv()

    barrier = pltpu.get_barrier_semaphore()
    peers = [at_x(x_up), at_x(x_down), at_z(z_up), at_z(z_down), by_i, by_t, sib]
    for dev in peers:
        pl.semaphore_signal(barrier, inc=1, device_id=dev, device_id_type=MESH)

    def block(k):
        return pl.ds(pl.multiple_of(k * R, R), R)

    def pair(p):
        return pl.ds(pl.multiple_of(p * 2 * R, 2 * R), 2 * R)

    def half(k, h):
        return pl.ds(pl.multiple_of(k * R + h * H, H), H)

    def islot(cc, b, xx):
        return cc * 2 * N + b * N + xx

    def tslot(o, zz):
        return o * N + zz

    imine, tmine = islot(c, yb, x), tslot(yo, z)
    img[block(imine), :] = unit_rows(img_ref[...])[0].astype(jnp.bfloat16)
    txt[block(tmine), :] = unit_rows(txt_ref[...])[0].astype(jnp.bfloat16)
    scale = jnp.exp(jnp.full((1, 1), scale_ref[0], jnp.float32))
    scale2 = scale * LOG2E
    pl.semaphore_wait(barrier, len(peers))

    def iview(k, h):
        return img.at[half(k, h), :]

    def tview(k, h):
        return txt.at[half(k, h), :]

    def igo(k, h, dev):
        go(iview(k, h), iview(k, h), g_r.at[k, h], dev)

    def tgo(k, h, dev):
        go(tview(k, h), tview(k, h), t_r.at[k, h], dev)

    def itake(k, h):
        take(iview(k, h), g_r.at[k, h])

    def ttake(k, h):
        take(tview(k, h), t_r.at[k, h])

    igo(imine, 0, by_i)
    tgo(tmine, 0, by_t)
    for h in (1, 0):
        for v, w in ((x_up, z_up), (x_down, z_down)):
            igo(imine, h, at_x(v))
            tgo(tmine, h, at_z(w))
    igo(imine, 1, by_i)
    tgo(tmine, 1, by_t)
    for h in range(2):
        igo(imine, h, sib)

    def ipass(b, v, h, devs):
        k = islot(c, b, v)
        itake(k, h)
        for dev in devs + [sib]:
            igo(k, h, dev)

    def tpass(o, v, h, devs):
        k = tslot(o, v)
        ttake(k, h)
        for dev in devs:
            tgo(k, h, dev)

    ipass(yb, x_down, 1, [at_x(x_up), by_i])
    tpass(yo, z_down, 1, [at_z(z_up), by_t])
    ipass(1 - yb, x, 0, [at_x(x_up), at_x(x_down)])
    tpass(1 - yo, z, 0, [at_z(z_up), at_z(z_down)])
    ipass(yb, x_up, 1, [by_i])
    tpass(yo, z_up, 1, [by_t])
    ipass(yb, x_up, 0, [at_x(x_down)])
    tpass(yo, z_up, 0, [at_z(z_down)])
    ipass(yb, x_down, 0, [])
    tpass(yo, z_down, 0, [])
    ipass(yb, turn(x, 2), 1, [by_i])
    tpass(yo, turn(z, 2), 1, [by_t])
    ipass(1 - yb, turn(x, 3 - 2 * c), 0, [at_x(turn(x, 1 + 2 * c))])
    tpass(1 - yo, turn(z, 3 - 2 * c), 0, [at_z(turn(z, 1 + 2 * c))])
    ipass(yb, turn(x, 2), 0, [])
    tpass(yo, turn(z, 2), 0, [])

    def tile_logits(q, o):
        rows = pl.ds(pl.multiple_of(q * N * R, N * R), N * R)
        cols = pl.ds(pl.multiple_of(o * N * R, N * R), N * R)
        l = scale2 * lax.dot_general(
            img[rows, :], txt[cols, :], (((1,), (1,)), ((), ())), preferred_element_type=jnp.float32
        )
        logit[rows, cols] = l
        return q, o, cols, l

    def tile_lse(q, o, cols, l):
        rmax = jnp.max(l, axis=1, keepdims=True)
        cmax = jnp.max(l, axis=0, keepdims=True)
        rsum = jnp.sum(jnp.exp2(l - rmax), axis=1, keepdims=True)
        csum = jnp.sum(jnp.exp2(l - cmax), axis=0, keepdims=True)
        rlse = rmax + jnp.log(rsum) * LOG2E
        line = jnp.broadcast_to(rlse, (N * R, R)).T[:1, :]
        for i in range(2):
            rowl[o, pl.ds(2 * q + i, 1), :] = line[:, i * 2 * R : (i + 1) * 2 * R]
        coll[q, :, cols] = cmax + jnp.log(csum) * LOG2E

    def sib_blocks(b):
        for v in range(N):
            for h in range(2):
                itake(islot(1 - c, b, v), h)

    def spot_of(i):
        return lax.rem(c + i, 2) * 2 + lax.rem(yb + i // 4, 2), lax.rem(yo + i // 2, 2)

    def tile_step(i, carry):
        @pl.when(i == 2)
        def _():
            sib_blocks(1 - yb)

        made = [tile_logits(*spot_of(2 * i + u)) for u in range(2)]
        for one in made:
            tile_lse(*one)
        return carry

    tile_lse(*tile_logits(*spot_of(0)))
    sib_blocks(yb)
    tile_lse(*tile_logits(*spot_of(1)))
    ipass(1 - yb, x, 1, [])
    for v in (x_down, x_up):
        ipass(1 - yb, v, 1, [])
    ipass(1 - yb, turn(x, 1 + 2 * c), 0, [])
    ipass(1 - yb, turn(x, 2), 1, [])
    ipass(1 - yb, turn(x, 2), 0, [])
    for v in (z, z_down, z_up, turn(z, 2)):
        tpass(1 - yo, v, 1, [])
    tpass(1 - yo, turn(z, 1 + 2 * c), 0, [])
    tpass(1 - yo, turn(z, 2), 0, [])
    lax.fori_loop(1, N, tile_step, 0)

    rowp[c] = lse2([rowl[0], rowl[1]])
    go(rowp.at[c], rowp.at[c], rp_r.at[c], sib)
    ime, tme = yb * N + x, yo * N + z
    colz[tme] = lse2([coll[q] for q in range(N)])
    for dev in same_t:
        go(colz.at[tme], colz.at[tme], cz_r.at[tme], dev)
    take(rowp.at[1 - c], rp_r.at[1 - c])
    rowx[ime] = lse2([rowp[0], rowp[1]])
    for dev in same_i:
        go(rowx.at[ime], rowx.at[ime], rx_r.at[ime], dev)

    def others(b, v):
        return [b * N + turn(v, d) for d in range(1, N)] + [(1 - b) * N + turn(v, d) for d in range(N)]

    for t in others(yo, z):
        take(colz.at[t], cz_r.at[t])
    coll[0] = lse2([colz[v] for v in range(2 * N)])
    for t in others(yb, x):
        take(rowx.at[t], rx_r.at[t])
    rowl[0] = lse2([rowx[v] for v in range(2 * N)])

    lane = lax.broadcasted_iota(jnp.int32, (8, R), 1)

    def meets(k):
        irow = k % N * 2 + k // (2 * N)
        icol = (yo * 2 + k // N % 2) * N + z
        trow, tcol = icol % (2 * N), irow * 2 + icol // (2 * N)
        ty = tcol // N
        here = jnp.logical_and(trow == row, jnp.logical_or(ty == y, ty == yt))
        return here, tslot(ty // 2, tcol % N)

    def delta_part(p, total):
        l = logit[pair(p), :]
        rcol = jnp.broadcast_to(rowl[0, pl.ds(p, 1), :], (R, 2 * R)).T[:, :1]
        target = lax.broadcasted_iota(jnp.int32, (2 * R, 1), 0)
        offs = []
        for i in range(2):
            here, slot = meets(2 * p + i)
            offs.append(jnp.where(here, (slot - i) * R, -4 * TEXTS))
        target = target + jnp.where(target < R, offs[0], offs[1])
        twice = jnp.where(lax.broadcasted_iota(jnp.int32, (2 * R, TEXTS), 1) == target, 2.0, 0.0)
        d = jnp.exp2(l - rcol) + jnp.exp2(l - coll[0]) - twice
        total = total + jnp.sum(d * l, axis=0, keepdims=True)
        low = d.astype(jnp.bfloat16)
        delta[pair(p), :] = low
        return low, total

    def image_part(low):
        return jnp.dot(low, txt[...], preferred_element_type=jnp.float32)

    def sum_go(level, at, devs):
        for dev in devs:
            go(sums.at[level, at], sums.at[level, at], su_r.at[level, at], dev)

    def sum_take(level, at):
        take(sums.at[level, at], su_r.at[level, at])

    ring_me, pair_me = (x, z), (yb, yo)
    ring_at, partner = (at_x, at_z), (by_i, by_t)
    stages = (stage_i, stage_t)

    def h0_copy(m, g, b, v):
        return send(
            stages[m].at[half(g, 0), :], a0.at[m, ring_me[m], b], pa0_s.at[m, g],
            pa0_r.at[m, ring_me[m], b], ring_at[m](v),
        )

    def h1_copy(m, g, v):
        return send(stages[m].at[half(g, 1), :], a1.at[m, v], pa1_s.at[m, g], pa1_r.at[m, v], partner[m])

    def spot(m, i):
        b = pair_me[m] if i // 2 else 1 - pair_me[m]
        near = ring_me[m] // 2
        return b, near if i % 2 else 1 - near

    def order(m, i):
        b, half_ring = spot(m, i)
        return b * 2 + half_ring

    def twin(m):
        return ring_me[m] + 1 - ring_me[m] % 2 * 2

    def emit(m, i, part):
        b, half_ring = spot(m, i)
        stages[m][pair(order(m, i)), :] = part.astype(jnp.bfloat16)
        for t in range(2):
            v = 2 * half_ring + t
            if i % 2:
                own0[m, i // 2, t] = part[t * R : t * R + H, :]
            else:
                h0_copy(m, b * N + v, b, v).start()
            if i // 2:
                own1[m, v] = part[t * R + H : (t + 1) * R, :]
            else:
                h1_copy(m, b * N + v, v).start()
        if i % 2:
            h0_copy(m, b * N + twin(m), b, twin(m)).start()

    def sib_copy(j):
        return send(stage_s.at[pair(j), :], stage_c.at[pair(j), :], qc_s.at[j], qc_r.at[j], sib)

    def sib_part(i, total):
        j = order(0, i)
        low, total = delta_part((1 - c) * N + j, total)
        stage_s[pair(j), :] = image_part(low).astype(jnp.bfloat16)
        return total

    total = jnp.zeros((1, TEXTS), jnp.float32)
    for i in range(2):
        total = sib_part(i, total)
    for i in range(2):
        sib_copy(order(0, i)).start()
    for i in range(2, N):
        total = sib_part(i, total)

    def image_emit(i, parts):
        for u in range(2):
            j = order(0, i + u)
            sib_copy(j).wait_recv()
            emit(0, i + u, parts[u] + stage_c[pair(j), :].astype(jnp.float32))

    def text_emit(i, count):
        parts = [
            lax.dot_general(
                delta[:, pair(order(1, i + u))], img[...], (((0,), (0,)), ((), ())),
                preferred_element_type=jnp.float32,
            )
            for u in range(count)
        ]
        for u in range(count):
            emit(1, i + u, parts[u])

    parts = []
    for i in range(2):
        low, total = delta_part(c * N + order(0, i), total)
        parts.append(image_part(low))
    for i in range(2, N):
        total = delta_part(c * N + order(0, i), total)[1]
    for i in range(2, N):
        sib_copy(order(0, i)).start()
    image_emit(0, parts)
    sums[0, c] = jnp.where(lane == 1, jnp.sum(total, axis=1, keepdims=True), jnp.zeros((8, R), jnp.float32))
    eye = lax.broadcasted_iota(jnp.int32, (R, R), 0) == lax.broadcasted_iota(jnp.int32, (R, R), 1)

    def loss_step(k, carry):
        here, slot = meets(k)

        @pl.when(here)
        def _():
            cols = block(slot)
            both = rowl[0, pl.ds(k // 2, 1), :]
            rl = jnp.where(k % 2 == 0, both[:, :R], both[:, R:])
            pairs = jnp.sum(jnp.where(eye, logit[block(k), cols], 0.0), axis=0, keepdims=True)
            part = jnp.sum(rl + coll[0, :, cols] - 2.0 * pairs, axis=1, keepdims=True)
            sums[0, c] = sums[0, c] + jnp.where(lane == 0, part, 0.0)

        return carry

    lax.fori_loop(0, N * N, loss_step, 0)
    sum_go(0, c, [sib])

    text_emit(0, 1)
    text_emit(1, 1)
    sum_take(0, 1 - c)
    sums[1, ime] = sums[0, 0] + sums[0, 1]
    sum_go(1, ime, same_i)
    image_emit(2, [image_part(delta[pair(c * N + order(0, i)), :]) for i in range(2, N)])
    text_emit(2, 2)


    def h0_sum(m, i):
        b = pair_me[m] if i else 1 - pair_me[m]
        acc = own0[m, i, ring_me[m] % 2]
        for d in range(1, N):
            s = turn(ring_me[m], d)
            take(a0.at[m, s, b], pa0_r.at[m, s, b])
            acc = acc + a0[m, s, b].astype(jnp.float32)
        return acc

    def h1_sum(m, v):
        take(a1.at[m, v], pa1_r.at[m, v])
        return own1[m, v] + a1[m, v].astype(jnp.float32)

    def second0(m):
        sb[m, N] = h0_sum(m, 0).astype(jnp.bfloat16)
        go(sb.at[m, N], b0.at[m], pb0_r.at[m], partner[m])

    def second1(m, v):
        sb[m, v] = h1_sum(m, v).astype(jnp.bfloat16)
        go(sb.at[m, v], b1.at[m, ring_me[m]], pb1_r.at[m, ring_me[m]], ring_at[m](v))

    def far_blocks(m):
        v = 2 - ring_me[m] // 2 * 2
        return v, v + 1

    for v in far_blocks(0):
        second1(0, v)
    for t in others(yb, x):
        sum_take(1, t)
    acc = sums[1, 0]
    for v in range(1, 2 * N):
        acc = acc + sums[1, v]
    sums[2, tme] = acc
    sum_go(2, tme, same_t)
    for v in far_blocks(1):
        second1(1, v)
    second1(0, twin(0))
    second0(0)
    second1(1, twin(1))
    second0(1)
    for m in range(2):
        fin[m, 0] = h0_sum(m, 1)
        fin[m, 1] = h1_sum(m, ring_me[m])

    factor = scale * (1.0 / (2.0 * TEXTS * N * N))
    for m in range(2):
        take(b0.at[m], pb0_r.at[m])
        acc = fin[m, 0] + b0[m].astype(jnp.float32)
        sum_ref[m, :H, :] = factor * acc
        acc = fin[m, 1]
        for d in range(1, N):
            s = turn(ring_me[m], d)
            take(b1.at[m, s], pb1_r.at[m, s])
            acc = acc + b1[m, s].astype(jnp.float32)
        sum_ref[m, H:, :] = factor * acc
    for t in others(yo, z):
        sum_take(2, t)
    whole = sums[2, 0]
    for v in range(1, 2 * N):
        whole = whole + sums[2, v]
    whole = whole * (LN2 / (2.0 * TEXTS * N * N))
    whole_ref[...] = whole

    for copy in started:
        copy.wait_send()

    for m in range(2):
        for b in range(2):
            for d in range(1, N):
                v = turn(ring_me[m], d)
                h0_copy(m, b * N + v, b, v).wait_send()
        for v in range(N):
            h1_copy(m, (1 - pair_me[m]) * N + v, v).wait_send()
    for j in range(N):
        sib_copy(j).wait_send()


def finish(img_ref, txt_ref, sum_ref, whole_ref, gi_ref, gt_ref, loss_ref, gs_ref):
    gi_ref[...] = project(img_ref[...], sum_ref[0])
    gt_ref[...] = project(txt_ref[...], sum_ref[1])
    whole = whole_ref[...]
    lane = lax.broadcasted_iota(jnp.int32, (8, R), 1)
    top = lax.broadcasted_iota(jnp.int32, (8, R), 0) == 0
    loss_ref[0] = jnp.sum(jnp.where(jnp.logical_and(top, lane == 0), whole, 0.0))
    gs_ref[0] = jnp.sum(jnp.where(jnp.logical_and(top, lane == 1), whole, 0.0))


def local(images, texts, log_scale):
    f32, bf16 = jnp.float32, jnp.bfloat16
    dma = pltpu.SemaphoreType.DMA
    vmem = pl.BlockSpec(memory_space=pltpu.VMEM)
    smem = pl.BlockSpec(memory_space=pltpu.SMEM)
    sums, whole = pl.pallas_call(
        kernel,
        out_shape=(jax.ShapeDtypeStruct((2, R, E), f32), jax.ShapeDtypeStruct((8, R), f32)),
        in_specs=[vmem, vmem, smem],
        out_specs=(vmem, vmem),
        scratch_shapes=[
            pltpu.VMEM((IMAGES, E), bf16),
            pltpu.VMEM((TEXTS, E), bf16),
            pltpu.VMEM((IMAGES, TEXTS), f32),
            pltpu.VMEM((IMAGES, TEXTS), bf16),
            pltpu.VMEM((TEXTS, E), bf16),
            pltpu.VMEM((TEXTS, E), bf16),
            pltpu.VMEM((TEXTS, E), bf16),
            pltpu.VMEM((TEXTS, E), bf16),
            pltpu.VMEM((2, 2, 2, H, E), f32),
            pltpu.VMEM((2, N, H, E), f32),
            pltpu.VMEM((2, 2, H, E), f32),
            pltpu.VMEM((2, N, 2, H, E), bf16),
            pltpu.VMEM((2, N, H, E), bf16),
            pltpu.VMEM((2, N + 1, H, E), bf16),
            pltpu.VMEM((2, H, E), bf16),
            pltpu.VMEM((2, N, H, E), bf16),
            pltpu.VMEM((2, PAIRS, 2 * R), f32),
            pltpu.VMEM((2, PAIRS, 2 * R), f32),
            pltpu.VMEM((2 * N, PAIRS, 2 * R), f32),
            pltpu.VMEM((N, 1, TEXTS), f32),
            pltpu.VMEM((2 * N, 1, TEXTS), f32),
            pltpu.VMEM((3, 2 * N, 8, R), f32),
            dma((96,)),
            dma((N * N, 2)),
            dma((2 * N, 2)),
            dma((2,)), dma((2 * N,)), dma((2 * N,)),
            dma((N,)), dma((N,)),
            dma((2, 2 * N)), dma((2, 2 * N)),
            dma((2, N, 2)), dma((2, N)),
            dma((2,)), dma((2, N)),
            dma((3, 2 * N)),
        ],
        compiler_params=pltpu.CompilerParams(
            collective_id=0, has_side_effects=True, vmem_limit_bytes=56 * 1024 * 1024
        ),
    )(images, texts, log_scale.reshape(1))
    gi, gt, loss, gs = pl.pallas_call(
        finish,
        out_shape=(
            jax.ShapeDtypeStruct((R, E), f32),
            jax.ShapeDtypeStruct((R, E), f32),
            jax.ShapeDtypeStruct((1,), f32),
            jax.ShapeDtypeStruct((1,), f32),
        ),
        in_specs=[vmem, vmem, vmem, vmem],
        out_specs=(vmem, vmem, smem, smem),
    )(images, texts, sums, whole)
    return gi, gt, loss.reshape(()), gs.reshape(())


def solution(mesh):
    placed = (P(("row", "col"), None), P(("col", "row"), None), P())
    return jax.shard_map(
        local,
        mesh=mesh,
        in_specs=placed,
        out_specs=(P(("row", "col"), None), P(("col", "row"), None), P(), P()),
        check_vma=False,
    )
```
